32 devices in a mesh: dp: 2 (over y), space: 16 (over z, x, core).
Axes of the slice: x: 2, y: 2, z: 4, core: 2. Of those that a mesh axis runs over, the one named last changes fastest.
Arguments:
- inputs: bfloat16 [2, 16, 48, 4096], P('dp', 'space'), may hold values from -6 to 6
- cotangent: bfloat16 [2, 16, 48, 4096], P('dp', 'space'), may hold values from -6 to 6
- conv_one: bfloat16 [9, 48, 48], replicated, may hold values from -0.3125 to 0.3125
- bias_one: float32 [48], replicated, may hold values from -3 to 3
- conv_two: bfloat16 [9, 48, 48], replicated, may hold values from -0.3125 to 0.3125
- bias_two: float32 [48], replicated, may hold values from -3 to 3
- neighbours: int32 [16, 4, 3], replicated, may hold values from 0 to 15, as said below
- corner_rule: int32 [16, 4], replicated, may hold values from 0 to 2
Outputs:
- output: bfloat16 [2, 16, 48, 4096], P('dp', 'space')
- grad_in: bfloat16 [2, 16, 48, 4096], P('dp', 'space')
- grad_conv_one: float32 [9, 48, 48], P(None, 'dp')
- grad_bias_one: float32 [48], P('dp')
- grad_conv_two: float32 [9, 48, 48], P(None, 'dp')
- grad_bias_two: float32 [48], P('dp')
The draws below stay inside these ranges and needn't reach their ends.
Inputs may be any that keep to these rules, and one draw needn't show every extreme that they name: Slot neighbours[t, e, 0] of a tile on the device block d (tiles d * 1 to d + 1 - 1) lies on block d - 1, d + 4, d + 1, d - 4 (cyclically over the 16 blocks) for e = 0, 1, 2, 3; neighbours[t, e, 1] and neighbours[t, e, 2] are 0 to 3.
All inputs are finite; a program needn't handle non-finite values.
Results may differ from the reference program's by a relative error of at most 0.009.
Values may be sent and summed in bfloat16 or wider, within the bound.
No kernel may reach another device: no remote copies, remote signals or barrier semaphores. Data moves between devices by JAX's collectives and lax.ppermute only.
A program may use at most 64 MiB of HBM per device.

```python
import jax
import jax.numpy as jnp
from jax import lax

C = 48
S = 64
TILE_DEV = 1
P_SIZE = 4096
TILES = 16
BATCH = 2
HOP = 4


def permute_block(block_key):
    return jax.random.permutation(block_key, TILE_DEV)


def draw_neighbours(key, part):
    devices = TILES // TILE_DEV
    slot_ids = jnp.arange(TILES, dtype=jnp.int32)
    device_of = slot_ids // TILE_DEV
    local_ids = slot_ids % TILE_DEV
    offsets = (-1, HOP, 1, -HOP)
    columns = []
    for edge_id in range(4):
        block_keys = jax.random.split(jax.random.fold_in(key, edge_id), devices)
        perms = jax.vmap(permute_block)(block_keys).astype(jnp.int32)
        source_device = (device_of + offsets[edge_id]) % devices
        columns.append(source_device * TILE_DEV + perms[device_of, local_ids])
    slots = jnp.stack(columns, axis=1)
    edges = jax.random.randint(jax.random.fold_in(key, 10), (TILES, 4), 0, 4, dtype=jnp.int32)
    rotations = jax.random.randint(jax.random.fold_in(key, 11), (TILES, 4), 0, 4, dtype=jnp.int32)
    return jnp.stack([slots, edges, rotations], axis=2).astype(jnp.int32)


def set_ends(values, rng, low, top_value):
    index_at = [jax.random.randint(jax.random.fold_in(rng, axis), (), 0, length) for axis, length in enumerate(values.shape)]
    main_axis = values.shape.index(max(values.shape))
    neighbour = index_at[:main_axis] + [(index_at[main_axis] + 1) % values.shape[main_axis]] + index_at[main_axis + 1:]
    return values.at[tuple(index_at)].set(low).at[tuple(neighbour)].set(top_value)


def level_of(rng, dims, shards, low, high):
    def one(position, parts):
        steps = jax.random.uniform(jax.random.fold_in(jax.random.fold_in(rng, 6), position), (parts,), jnp.float32, low / len(shards), high / len(shards))
        return jnp.repeat(jnp.exp(steps), dims[position] // parts).reshape((-1,) + (1,) * (len(dims) - position - 1))

    factor_of = one(*shards[0])
    for cut in shards[1:]:
        factor_of = factor_of * one(*cut)
    return factor_of


def scatter_about(key, shape, scale, most, cuts=(), kind=jnp.bfloat16):
    level = level_of(key, shape, cuts, -0.22, 0.18) if cuts else 1.0
    drawn = jax.random.normal(key, shape, jnp.float32) * scale * level
    return jnp.minimum(jnp.maximum(drawn, -most), most).astype(kind)


def setup_inputs(seed: int = 0) -> dict:
    key_list = jax.random.split(jax.random.key(seed), 9)
    return {
        "inputs": scatter_about(key_list[0], (BATCH, TILES, C, P_SIZE), 1.0, 6.0, ((0, 2), (1, 16))),
        "cotangent": scatter_about(key_list[1], (BATCH, TILES, C, P_SIZE), 1.0, 6.0, ((0, 2), (1, 16))),
        "conv_one": scatter_about(key_list[2], (9, C, C), (9 * C) ** -0.5, 0.3125),
        "bias_one": scatter_about(key_list[3], (C,), 0.5, 3.0, (), jnp.float32),
        "conv_two": scatter_about(key_list[4], (9, C, C), (9 * C) ** -0.5, 0.3125),
        "bias_two": scatter_about(key_list[5], (C,), 0.5, 3.0, (), jnp.float32),
        "neighbours": draw_neighbours(jax.random.fold_in(key_list[8], 71), 0),
        "corner_rule": set_ends(jax.random.randint(key_list[7], (TILES, 4), 0, 3), jax.random.fold_in(key_list[7], 1), 0, 2).astype(jnp.int32),
    }


def lines_of(tile_image):
    return jnp.stack([tile_image[..., 0, :], tile_image[..., :, -1], tile_image[..., -1, :], tile_image[..., :, 0]], axis=2)

def assemble(tile_image, edge_lines, tile_rules):
    top_line = edge_lines[:, :, 0]
    right_line = edge_lines[:, :, 1]
    bottom_line = edge_lines[:, :, 2]
    left_line = edge_lines[:, :, 3]
    pairs = ((top_line[..., 0], left_line[..., 0]), (top_line[..., -1], right_line[..., 0]), (bottom_line[..., 0], left_line[..., -1]), (bottom_line[..., -1], right_line[..., -1]))
    corners = []
    for corner_id in range(4):
        first_value, second_value = pairs[corner_id]
        rule_now = tile_rules[:, corner_id][None, :, None]
        mean_value = ((first_value.astype(jnp.float32) + second_value.astype(jnp.float32)) * 0.5).astype(tile_image.dtype)
        corners.append(jnp.where(rule_now == 0, first_value, jnp.where(rule_now == 1, second_value, mean_value)))
    middle = jnp.concatenate([left_line[..., :, None], tile_image, right_line[..., :, None]], axis=-1)
    top_row = jnp.concatenate([corners[0][..., None], top_line, corners[1][..., None]], axis=-1)
    bottom_row = jnp.concatenate([corners[2][..., None], bottom_line, corners[3][..., None]], axis=-1)
    return jnp.concatenate([top_row[..., None, :], middle, bottom_row[..., None, :]], axis=-2)

def halo_ref(field, neighbours, corner_rule):
    batch_len, tile_count, channels, pixels = field.shape
    side_len = S
    tile_image = field.reshape(batch_len, tile_count, channels, side_len, side_len)
    all_lines = lines_of(tile_image).reshape(batch_len, tile_count * 4, channels, side_len)
    picked = all_lines[:, neighbours[:, :, 0] * 4 + neighbours[:, :, 1]]
    flip_mask = (neighbours[:, :, 2] == 1) | (neighbours[:, :, 2] == 2)
    picked = jnp.where(flip_mask[None, :, :, None, None], picked[..., ::-1], picked)
    return assemble(tile_image, picked, corner_rule)

def conv_apply(padded, weights):
    lead = padded.shape[:3]
    row_width = padded.shape[-1]
    side_len = row_width - 2
    out_span = side_len * row_width
    flat_pad = jnp.pad(padded.reshape(lead + (row_width * row_width,)), ((0, 0), (0, 0), (0, 0), (0, 2))).astype(jnp.float32)
    summed = jnp.zeros(lead[:2] + (weights.shape[1], out_span), jnp.float32)
    for tap_id in range(9):
        start_at = tap_id // 3 * row_width + tap_id % 3
        window = lax.slice_in_dim(flat_pad, start_at, start_at + out_span, axis=3)
        summed = summed + jnp.einsum('oc,btcq->btoq', weights[tap_id].astype(jnp.float32), window)
    return summed.reshape(lead[:2] + (weights.shape[1], side_len, row_width))[..., :side_len].reshape(lead[:2] + (weights.shape[1], side_len * side_len))

def spread_rows(grad, side_len):
    lead = grad.shape[:3]
    squared = grad.reshape(lead + (side_len, side_len))
    return jnp.pad(squared, ((0, 0), (0, 0), (0, 0), (0, 0), (0, 2))).reshape(lead + (side_len * (side_len + 2),))

def conv_transpose(grad, weights, side_len):
    lead = grad.shape[:2]
    row_width = side_len + 2
    out_span = side_len * row_width
    full_len = row_width * row_width + 2
    flat_grad = spread_rows(grad, side_len).astype(jnp.float32)
    summed = jnp.zeros(lead + (weights.shape[2], full_len), jnp.float32)
    for tap_id in range(9):
        start_at = tap_id // 3 * row_width + tap_id % 3
        placed = jnp.einsum('oc,btoq->btcq', weights[tap_id].astype(jnp.float32), flat_grad)
        summed = summed + jnp.pad(placed, ((0, 0), (0, 0), (0, 0), (start_at, full_len - out_span - start_at)))
    return summed[..., :row_width * row_width].reshape(lead + (weights.shape[2], row_width, row_width))

def weight_grad(grad, padded):
    lead = padded.shape[:3]
    row_width = padded.shape[-1]
    side_len = row_width - 2
    out_span = side_len * row_width
    flat_grad = spread_rows(grad, side_len).astype(jnp.float32)
    flat_pad = jnp.pad(padded.reshape(lead + (row_width * row_width,)), ((0, 0), (0, 0), (0, 0), (0, 2))).astype(jnp.float32)
    taps = []
    for tap_id in range(9):
        start_at = tap_id // 3 * row_width + tap_id % 3
        window = lax.slice_in_dim(flat_pad, start_at, start_at + out_span, axis=3)
        taps.append(jnp.einsum('btoq,btcq->oc', flat_grad, window))
    return jnp.stack(taps, axis=0)

def activate(values):
    return jax.nn.gelu(values, approximate=True)

def reference(inputs, cotangent, conv_one, bias_one, conv_two, bias_two, neighbours, corner_rule):

    def halo_linear(field):
        return halo_ref(field, neighbours, corner_rule)

    def one_sample(pair):
        sample_in = pair[0][None]
        sample_grad = pair[1][None]
        pad_in = halo_ref(sample_in, neighbours, corner_rule)
        pre_one = conv_apply(pad_in, conv_one) + bias_one[None, None, :, None]
        act_one = activate(pre_one).astype(jnp.bfloat16)
        pad_act = halo_ref(act_one, neighbours, corner_rule)
        output = (sample_in.astype(jnp.float32) + conv_apply(pad_act, conv_two) + bias_two[None, None, :, None]).astype(jnp.bfloat16)
        d_pad_act = conv_transpose(sample_grad, conv_two, S)
        pull_act = jax.vjp(halo_linear, act_one.astype(jnp.float32))[1]
        d_act = pull_act(d_pad_act)[0]
        pull_gelu = jax.vjp(activate, pre_one)[1]
        d_pre = pull_gelu(d_act)[0].astype(jnp.bfloat16)
        grad_two = weight_grad(sample_grad, pad_act)
        bias_grad_two = lax.optimization_barrier(jnp.sum(sample_grad.astype(jnp.float32), axis=(0, 1, 3)))
        grad_one = weight_grad(d_pre, pad_in)
        bias_grad_one = lax.optimization_barrier(jnp.sum(d_pre.astype(jnp.float32), axis=(0, 1, 3)))
        d_pad_in = conv_transpose(d_pre, conv_one, S)
        pull_in = jax.vjp(halo_linear, sample_in.astype(jnp.float32))[1]
        grad_in = (sample_grad.astype(jnp.float32) + pull_in(d_pad_in)[0]).astype(jnp.bfloat16)
        return (output[0], grad_in[0], grad_one, bias_grad_one, grad_two, bias_grad_two)
    results = lax.map(one_sample, (inputs, cotangent))
    return (results[0], results[1], lax.optimization_barrier(jnp.sum(results[2], axis=0)), lax.optimization_barrier(jnp.sum(results[3], axis=0)), lax.optimization_barrier(jnp.sum(results[4], axis=0)), lax.optimization_barrier(jnp.sum(results[5], axis=0)))
```

```python
import functools
import math

import jax
import jax.numpy as jnp
from jax import lax
from jax.experimental import pallas as pl
from jax.experimental.pallas import tpu as pltpu
from jax.sharding import PartitionSpec as P

BF = jnp.bfloat16
F32 = jnp.float32
C = 48
SIDE = 64
PIX = SIDE * SIDE
LANES = 128
TILES = PIX // LANES
LINE_AT = (64, 0, 0, 0)
USER_AT = (0, 64, 64, 64)

VMEM = pl.BlockSpec(memory_space=pltpu.VMEM)
SMEM = pl.BlockSpec(memory_space=pltpu.SMEM)


def tap_of(edge, step):
    return (step, 3 * step + 2, 6 + step, 3 * step)[edge]


def offsets_of(spaces):
    return (-1, spaces // 4, 1, -(spaces // 4))


def dot(a, b):
    return jnp.dot(a, b, preferred_element_type=F32)


def dot_nt(a, b):
    return lax.dot_general(a, b, (((1,), (1,)), ((), ())), preferred_element_type=F32)


def iota(shape, axis):
    return lax.broadcasted_iota(jnp.int32, shape, axis)


def line_lanes(lane):
    z = lane - 128
    even = (z & 1) == 0
    left = jnp.where(z < 64, z, z - 63)
    right = jnp.where(z < 63, z + 2, jnp.where(z < 127, z - 63, 1))
    line = jnp.where(lane < 64, 0, jnp.where(lane < 128, 2, jnp.where(even, 3, 1)))
    place = jnp.where(lane < 64, lane, jnp.where(lane < 128, lane - 64, jnp.where(even, left, right)))
    return line, place


def lane_masks():
    lane = iota((C, LANES), 1) & 63
    return lane == 0, lane == 63


def tile(ref, t):
    return ref[:, t * LANES : (t + 1) * LANES]


def lines_from(tiles, first, last):
    total = tiles[0]
    for t in range(1, TILES):
        total = total + pltpu.roll(tiles[t], 2 * t, 1)
    low = iota((C, LANES), 1) < 64
    rows = jnp.where(low, first, last)
    return jnp.concatenate([rows, total], axis=1).astype(BF)


def edge_only(values):
    at_left, at_right = lane_masks()
    return jnp.where(at_left | at_right, values, 0.0)


def send_matrices(tables, rules, me, spaces):
    row = iota((256, LANES), 0)
    lane = iota((256, LANES), 1)
    line, place = line_lanes(row)
    out = []
    for edge, offset in enumerate(offsets_of(spaces)):
        target = lax.rem(me - offset + spaces, spaces)
        k = tables[target, edge, 1]
        r = tables[target, edge, 2]
        turned = (r == 1) | (r == 2)
        want = jnp.where(turned, 63 - place, place)
        top = (line == k) & (lane - LINE_AT[edge] == want)
        own = (line == (edge + 2) % 4) & (lane - USER_AT[edge] == place)
        out.append(jnp.concatenate([jnp.where(top, 1.0, 0.0), jnp.where(own, 1.0, 0.0)], axis=0).astype(BF))
    return out


def my_space():
    return lax.axis_index("space")


def send_kernel(spaces, tables, rules, x_ref, g_ref, *outs):
    me = my_space()

    def lines(ref):
        tiles = [edge_only(tile(ref, t).astype(F32)) for t in range(TILES)]
        return lines_from(tiles, tile(ref, 0).astype(F32), tile(ref, TILES - 1).astype(F32))

    both = jnp.concatenate([lines(x_ref), lines(g_ref)], axis=1)
    for out, matrix in zip(outs, send_matrices(tables, rules, me, spaces)):
        out[...] = dot(both, matrix).astype(BF)


def weights_of(rules, where, corner):
    rule = rules[where, corner]
    first = jnp.where(rule == 0, 1.0, jnp.where(rule == 1, 0.0, 0.5)).astype(F32)
    return first, 1.0 - first


def user_matrix(tables, rules, me, spaces, edge, step):
    used = (edge + 2) % 4
    user = lax.rem(me + offsets_of(spaces)[edge] + spaces, spaces)
    k = tables[user, used, 1]
    r = tables[user, used, 2]
    turned = (r == 1) | (r == 2)
    q = iota((LANES, 256), 0) - USER_AT[edge]
    line, place = line_lanes(iota((LANES, 256), 1))
    want = jnp.where(turned, 63 - place, place)
    value = jnp.where(q == want + 1 - step, 1.0, 0.0)
    which = used % 2
    corners = ((0, 1), (1, 3), (2, 3), (0, 2))[used]
    if step == 0:
        weight = weights_of(rules, user, corners[0])[which]
        value = value + jnp.where((want == 0) & (q == 0), weight, 0.0)
    if step == 2:
        weight = weights_of(rules, user, corners[1])[which]
        value = value + jnp.where((want == 63) & (q == 63), weight, 0.0)
    return jnp.where((line == k) & (q >= 0) & (q < 64), value, 0.0).astype(BF)


def halo_matrix(rules, me, step):
    row = iota((512, 256), 0)
    line, place = line_lanes(iota((1, 256), 1))
    at = place + step - 1
    base = line * 128 + jnp.where(line == 0, 64, 0)
    inside = (at >= 0) & (at < 64)
    value = jnp.where(inside & (row == base + at), 1.0, 0.0)
    side = (line == 3) | (line == 1)
    left = line == 3
    base0, base1, base2, base3 = 64, 128, 256, 384
    if step != 1:
        if step == 0:
            active = side & (place == 0)
            row_a = jnp.where(left, base0, base0 + 63)
            row_b = jnp.where(left, base3, base1)
            pair = (0, 1)
        else:
            active = side & (place == 63)
            row_a = jnp.where(left, base2, base2 + 63)
            row_b = jnp.where(left, base3 + 63, base1 + 63)
            pair = (2, 3)
        fl, sl = weights_of(rules, me, pair[0])
        fr, sr = weights_of(rules, me, pair[1])
        value = value + jnp.where(active & (row == row_a), jnp.where(left, fl, fr), 0.0)
        value = value + jnp.where(active & (row == row_b), jnp.where(left, sl, sr), 0.0)
    return value.astype(BF)


def half_shift(dst, ref, before, after):
    low = iota((C, LANES), 1) < 64
    for t in range(TILES + 1):
        here = tile(ref, t) if t < TILES else after
        prev = tile(ref, t - 1) if t > 0 else before
        mixed = jnp.where(low, here.astype(F32), prev.astype(F32))
        dst[:, t * LANES : (t + 1) * LANES] = pltpu.roll(mixed, 64, 1).astype(BF)


def stack_of(half, ref, start, width):
    at = start * LANES
    size = width * LANES
    return jnp.concatenate(
        [half[:, at : at + size], ref[:, at : at + size], half[:, at + LANES : at + LANES + size]], axis=0
    )


def conv_tiles(weights, half, ref, columns, visit):
    at_left, at_right = lane_masks()
    for chunk in range(TILES // 2):
        taps = dot(weights, stack_of(half, ref, 2 * chunk, 2))
        for part in range(2):
            t = 2 * chunk + part
            lanes = slice(part * LANES, (part + 1) * LANES)
            side = 0.0 if columns is None else pltpu.roll(columns, (LANES - 2 * t) % LANES, 1)
            left = jnp.where(at_left, side, pltpu.roll(taps[0:C, lanes], 1, 1))
            right = jnp.where(at_right, side, pltpu.roll(taps[2 * C : 3 * C, lanes], LANES - 1, 1))
            visit(t, taps[C : 2 * C, lanes] + left + right)


def prepare_kernel(spaces, tables, rules, x_ref, g_ref, wt_ref, d_act, g_side, x_side, route, halo, half):
    me = my_space()
    zero = jnp.zeros((C, LANES), BF)
    half_shift(half, g_ref, zero, zero)

    def visit(t, value):
        d_act[:, t * LANES : (t + 1) * LANES] = value

    conv_tiles(wt_ref[...], half, g_ref, None, visit)
    at_left, at_right = lane_masks()
    for t in range(TILES):
        at = slice(t * LANES, (t + 1) * LANES)
        g = tile(g_ref, t).astype(F32)
        x = tile(x_ref, t).astype(F32)
        g_side[0:C, at] = jnp.where(at_right, 0.0, pltpu.roll(g, LANES - 1, 1)).astype(BF)
        g_side[C : 2 * C, at] = jnp.where(at_left, 0.0, pltpu.roll(g, 1, 1)).astype(BF)
        x_side[0:C, at] = jnp.where(at_left, 0.0, pltpu.roll(x, 1, 1)).astype(BF)
        x_side[C : 2 * C, at] = jnp.where(at_right, 0.0, pltpu.roll(x, LANES - 1, 1)).astype(BF)
    for edge in range(4):
        for step in range(3):
            route[edge, :, step * 256 : (step + 1) * 256] = user_matrix(tables, rules, me, spaces, edge, step)
    for step in range(3):
        halo[:, step * 256 : (step + 1) * 256] = halo_matrix(rules, me, step)


def column_terms(weights, beside):
    stacked = jnp.concatenate([beside[:, s * 256 + 128 : (s + 1) * 256] for s in range(3)], axis=0)
    both = dot(jnp.concatenate([weights[0:C], weights[2 * C : 3 * C]], axis=0), stacked)
    even = (iota((C, LANES), 1) & 1) == 0
    return jnp.where(even, both[0:C], both[C : 2 * C])


def users_values(route, blocks):
    parts = []
    for edge in range(4):
        moved = dot(blocks[edge], route[edge]).astype(BF)
        parts += [moved[:, s * 256 : (s + 1) * 256] for s in range(3)]
    return jnp.concatenate(parts, axis=0)


def middle_kernel(
    spaces, tables, rules, x_ref, a0, a1, a2, a3, d_act, route, halo, wf, back, bias,
    act_ref, d_ref, p0, p1, p2, p3, beside_ref, users_ref, act_lines, d_lines, half,
):
    me = my_space()
    blocks = [a[...] for a in (a0, a1, a2, a3)]
    half_shift(half, x_ref, blocks[0], blocks[2])
    beside = dot(jnp.concatenate(blocks, axis=1), halo[...]).astype(BF)
    beside_ref[...] = beside
    columns = column_terms(wf[...], beside)
    users = users_values(route, blocks)
    users_ref[...] = users
    line_grads = dot(back[...], users)
    rows = line_grads[:, 0:LANES]
    sides = line_grads[:, LANES : 2 * LANES]
    low = iota((C, LANES), 1) < 64
    at_left, at_right = lane_masks()
    at_edge = at_left | at_right
    bias_now = jnp.broadcast_to(bias[...], (C, LANES))
    act_edges = []
    d_edges = []
    ends = {}

    def visit(t, value):
        at = slice(t * LANES, (t + 1) * LANES)
        pre = value + bias_now
        square = pre * pre
        inner = 0.7978845608028654 * pre * (1.0 + 0.044715 * square)
        wave = jnp.tanh(inner)
        cdf = 0.5 + 0.5 * wave
        slope = cdf + 0.5 * pre * (1.0 - wave * wave) * (0.7978845608028654 + 0.1070322243 * square)
        grad = d_act[:, at] + jnp.where(at_edge, pltpu.roll(sides, (LANES - 2 * t) % LANES, 1), 0.0)
        if t == 0:
            grad = grad + jnp.where(low, rows, 0.0)
        if t == TILES - 1:
            grad = grad + jnp.where(low, 0.0, rows)
        act = (pre * cdf).astype(BF)
        d_pre = (grad * slope).astype(BF)
        act_ref[:, at] = act
        d_ref[:, at] = d_pre
        act = act.astype(F32)
        d_pre = d_pre.astype(F32)
        act_edges.append(edge_only(act))
        d_edges.append(edge_only(d_pre))
        if t in (0, TILES - 1):
            ends[t] = (act, d_pre)

    conv_tiles(wf[...], half, x_ref, columns, visit)
    act_l = lines_from(act_edges, ends[0][0], ends[TILES - 1][0])
    d_l = lines_from(d_edges, ends[0][1], ends[TILES - 1][1])
    act_lines[...] = act_l
    d_lines[...] = d_l
    both = jnp.concatenate([act_l, d_l], axis=1)
    for out, matrix in zip((p0, p1, p2, p3), send_matrices(tables, rules, me, spaces)):
        out[...] = dot(both, matrix).astype(BF)


def grads_kernel(
    parts, x_ref, g_ref, act_ref, d_ref, g_side, x_side, beside, users, act_lines, d_lines, wt,
    sums, d_in, half_a, half_d, held_one, held_two, beside_one, beside_two,
):
    zero = jnp.zeros((C, LANES), BF)
    half_shift(half_a, act_ref, zero, zero)
    half_shift(half_d, d_ref, zero, zero)
    width = 4
    one = jnp.zeros((3 * C, 3 * C), F32)
    two = jnp.zeros((3 * C, 3 * C), F32)
    ones = jnp.zeros((C, 1), F32)
    twos = jnp.zeros((C, 1), F32)
    for start in range(0, TILES, width):
        at = slice(start * LANES, (start + width) * LANES)
        g_now = jnp.concatenate([g_side[0:C, at], g_ref[:, at], g_side[C : 2 * C, at]], axis=0)
        x_now = jnp.concatenate([x_side[0:C, at], x_ref[:, at], x_side[C : 2 * C, at]], axis=0)
        two = two + dot_nt(g_now, stack_of(half_a, act_ref, start, width))
        one = one + dot_nt(stack_of(half_d, d_ref, start, width), x_now)
        ones = ones + jnp.sum(d_ref[:, at].astype(F32), axis=1, keepdims=True)
        twos = twos + jnp.sum(g_ref[:, at].astype(F32), axis=1, keepdims=True)
    line, _ = line_lanes(iota((C, 256), 1))
    d_l = d_lines[...].astype(F32)
    by_edge = jnp.concatenate([jnp.where(line == e, d_l, 0.0) for e in range(4)], axis=0).astype(BF)
    side_one = dot_nt(by_edge, jnp.concatenate([beside[:, s * 256 : (s + 1) * 256] for s in range(3)], axis=0))
    held_one[...] = one
    held_two[...] = two
    beside_one[...] = side_one
    beside_two[...] = dot_nt(users[...], act_lines[...])
    share = C // parts
    for tap in range(9):
        a, b = tap // 3, tap % 3
        value_one = held_one[(2 - a) * C : (3 - a) * C, b * C : (b + 1) * C]
        value_two = held_two[b * C : (b + 1) * C, a * C : (a + 1) * C]
        for edge in range(4):
            for step in range(3):
                if tap_of(edge, step) == tap:
                    value_one = value_one + beside_one[edge * C : (edge + 1) * C, step * C : (step + 1) * C]
                    at = ((edge + 2) % 4) * 3 + step
                    value_two = value_two + beside_two[at * C : (at + 1) * C, :]
        tail = jnp.concatenate([ones, twos, jnp.zeros((C, 30), F32)], axis=1)
        whole = jnp.concatenate([value_one, value_two, tail], axis=1)
        for part in range(parts):
            sums[part, tap] = whole[part * share : (part + 1) * share].astype(BF)

    def visit(t, value):
        at = slice(t * LANES, (t + 1) * LANES)
        d_in[:, at] = value + g_ref[:, at].astype(F32)

    conv_tiles(wt[...], half_d, d_ref, None, visit)


def output_kernel(x_ref, act_ref, a0, a1, a2, a3, halo, wf, bias, out, half):
    blocks = [a[...] for a in (a0, a1, a2, a3)]
    half_shift(half, act_ref, blocks[0], blocks[2])
    beside = dot(jnp.concatenate(blocks, axis=1), halo[...]).astype(BF)
    columns = column_terms(wf[...], beside)
    bias_now = jnp.broadcast_to(bias[...], (C, LANES))

    def visit(t, value):
        at = slice(t * LANES, (t + 1) * LANES)
        out[:, at] = (value + bias_now + x_ref[:, at].astype(F32)).astype(BF)

    conv_tiles(wf[...], half, act_ref, columns, visit)


def grad_in_kernel(d_in, a0, a1, a2, a3, route, back, out):
    blocks = [a[...] for a in (a0, a1, a2, a3)]
    line_grads = dot(back[...], users_values(route, blocks))
    rows = line_grads[:, 0:LANES]
    sides = line_grads[:, LANES : 2 * LANES]
    low = iota((C, LANES), 1) < 64
    at_left, at_right = lane_masks()
    at_edge = at_left | at_right
    for t in range(TILES):
        at = slice(t * LANES, (t + 1) * LANES)
        value = d_in[:, at] + jnp.where(at_edge, pltpu.roll(sides, (LANES - 2 * t) % LANES, 1), 0.0)
        if t == 0:
            value = value + jnp.where(low, rows, 0.0)
        if t == TILES - 1:
            value = value + jnp.where(low, 0.0, rows)
        out[:, at] = value.astype(BF)


def call(kernel, outs, specs, args, scratch=(), flops=0, read=0):
    return pl.pallas_call(
        kernel,
        out_shape=[jax.ShapeDtypeStruct(shape, dtype) for shape, dtype in outs],
        in_specs=specs,
        out_specs=[VMEM] * len(outs),
        scratch_shapes=list(scratch),
        compiler_params=pltpu.CompilerParams(vmem_limit_bytes=32 * 1024 * 1024),
        cost_estimate=pl.CostEstimate(flops=flops, bytes_accessed=read, transcendentals=0),
    )(*args)


def exchange(blocks, spaces):
    arrived = []
    for block, offset in zip(blocks, offsets_of(spaces)):
        route = [((i + offset) % spaces, i) for i in range(spaces)]
        arrived.append(lax.ppermute(block, "space", route))
    return arrived


def paired(block, axis, distance):
    size = lax.axis_size(axis)
    return lax.ppermute(block, axis, [(i, i ^ distance) for i in range(size)])


def total_over_devices(sums, parts, spaces):
    me = lax.axis_index("dp")
    span = parts
    held = sums
    while span > 1:
        span //= 2
        upper = (me // span) % 2 == 1
        low, high = held[:span], held[span:]
        keep = jnp.where(upper, high, low)
        give = jnp.where(upper, low, high)
        got = paired(give, "dp", span)
        held = (keep.astype(F32) + got.astype(F32)).astype(BF)
    held = held[0]
    distance = 1
    while distance < spaces:
        got = paired(held, "space", distance)
        distance *= 2
        held = held.astype(F32) + got.astype(F32)
        if distance < spaces:
            held = held.astype(BF)
    return held


def conv_flops():
    return 2 * 9 * C * C * PIX


def on_device(inputs, cotangent, conv_one, bias_one, conv_two, bias_two, neighbours, corner_rule):
    parts = lax.axis_size("dp")
    spaces = lax.axis_size("space")
    x = inputs.reshape(C, PIX)
    g = cotangent.reshape(C, PIX)
    line = ((C, LANES), BF)
    image = ((C, PIX), BF)

    def forward(w):
        return w.reshape(3, 3, C, C).transpose(1, 2, 0, 3).reshape(3 * C, 3 * C)

    def backward(w):
        return w.reshape(3, 3, C, C)[::-1, ::-1].transpose(1, 3, 0, 2).reshape(3 * C, 3 * C)

    def returning(w):
        taps = [w[tap_of((edge + 2) % 4, step)].T for edge in range(4) for step in range(3)]
        return jnp.concatenate(taps, axis=1)

    sent = call(
        functools.partial(send_kernel, spaces), [line] * 4, [SMEM, SMEM, VMEM, VMEM],
        (neighbours, corner_rule, x, g), flops=10**6, read=10**6,
    )
    arrived = exchange(sent, spaces)
    half = pltpu.VMEM((C, PIX + LANES), BF)
    d_act, g_side, x_side, route, halo = call(
        functools.partial(prepare_kernel, spaces),
        [((C, PIX), F32), ((2 * C, PIX), BF), ((2 * C, PIX), BF), ((4, LANES, 768), BF), ((512, 768), BF)],
        [SMEM, SMEM, VMEM, VMEM, VMEM],
        (neighbours, corner_rule, x, g, backward(conv_two)), [half], flops=conv_flops(), read=4 * 10**6,
    )
    middle = call(
        functools.partial(middle_kernel, spaces),
        [image, image] + [line] * 4 + [((C, 768), BF), ((12 * C, 256), BF), ((C, 256), BF), ((C, 256), BF)],
        [SMEM, SMEM] + [VMEM] * 11,
        (neighbours, corner_rule, x, *arrived, d_act, route, halo, forward(conv_one), returning(conv_two),
         bias_one.reshape(C, 1)),
        [half], flops=conv_flops(), read=4 * 10**6,
    )
    act, d_pre = middle[:2]
    beside, users, act_lines, d_lines = middle[6:]
    again = exchange(middle[2:6], spaces)
    sums, d_in = call(
        functools.partial(grads_kernel, parts), [((parts, 9, C // parts, LANES), BF), ((C, PIX), F32)], [VMEM] * 11,
        (x, g, act, d_pre, g_side, x_side, beside, users, act_lines, d_lines, backward(conv_one)),
        [half, half, pltpu.VMEM((3 * C, 3 * C), F32), pltpu.VMEM((3 * C, 3 * C), F32),
         pltpu.VMEM((4 * C, 3 * C), F32), pltpu.VMEM((12 * C, C), F32)],
        flops=3 * conv_flops(), read=6 * 10**6,
    )
    (output,) = call(
        output_kernel, [image], [VMEM] * 9,
        (x, act, *again, halo, forward(conv_two), bias_two.reshape(C, 1)), [half],
        flops=conv_flops(), read=3 * 10**6,
    )
    (grad_in,) = call(
        grad_in_kernel, [image], [VMEM] * 7, (d_in, *again, route, returning(conv_one)),
        flops=10**6, read=3 * 10**6,
    )
    total = total_over_devices(sums, parts, spaces)
    shape = inputs.shape
    return (
        output.reshape(shape),
        grad_in.reshape(shape),
        total[:, :, 0:C],
        total[0, :, 2 * C],
        total[:, :, C : 2 * C],
        total[0, :, 2 * C + 1],
    )


def solution(mesh):
    tiles = P("dp", "space", None, None)
    return jax.shard_map(
        on_device,
        mesh=mesh,
        in_specs=(tiles, tiles, P(), P(), P(), P(), P(), P()),
        out_specs=(tiles, tiles, P(None, "dp", None), P("dp"), P(None, "dp", None), P("dp")),
        check_vma=False,
    )
```

```python
import functools

import jax
import jax.numpy as jnp
from jax import lax
from jax.experimental import pallas as pl
from jax.experimental.pallas import tpu as pltpu
from jax.sharding import PartitionSpec as P

BF = jnp.bfloat16
F32 = jnp.float32
C = 48
SIDE = 64
PIX = SIDE * SIDE
LANES = 128
TILES = PIX // LANES

VMEM = pl.BlockSpec(memory_space=pltpu.VMEM)
SMEM = pl.BlockSpec(memory_space=pltpu.SMEM)


def tap_of(edge, step):
    return (step, 3 * step + 2, 6 + step, 3 * step)[edge]


def offsets_of(spaces):
    return (-1, spaces // 4, 1, -(spaces // 4))


def dot(a, b):
    return jnp.dot(a, b, preferred_element_type=F32)


def dot_nt(a, b):
    return lax.dot_general(a, b, (((1,), (1,)), ((), ())), preferred_element_type=F32)


def iota(shape, axis):
    return lax.broadcasted_iota(jnp.int32, shape, axis)


def line_lanes(lane):
    z = lane - 128
    even = (z & 1) == 0
    left = jnp.where(z < 64, z, z - 63)
    right = jnp.where(z < 63, z + 2, jnp.where(z < 127, z - 63, 1))
    line = jnp.where(lane < 64, 0, jnp.where(lane < 128, 2, jnp.where(even, 3, 1)))
    place = jnp.where(lane < 64, lane, jnp.where(lane < 128, lane - 64, jnp.where(even, left, right)))
    return line, place


def lane_masks():
    lane = iota((C, LANES), 1) & 63
    return lane == 0, lane == 63


def tile(ref, t):
    return ref[:, t * LANES : (t + 1) * LANES]


def lines_from(tiles, first, last):
    total = tiles[0]
    for t in range(1, TILES):
        total = total + pltpu.roll(tiles[t], 2 * t, 1)
    low = iota((C, LANES), 1) < 64
    rows = jnp.where(low, first, last)
    return jnp.concatenate([rows, total], axis=1).astype(BF)


def edge_only(values):
    at_left, at_right = lane_masks()
    return jnp.where(at_left | at_right, values, 0.0)


def roles(spaces):
    me = lax.axis_index("space")
    return me, (me % 2) == 0, ((me // (spaces // 4)) % 2) == 0


def swap_edges(even, inner):
    return (
        jnp.where(even, 0, 2),
        jnp.where(even, 2, 0),
        jnp.where(inner, 3, 1),
        jnp.where(inner, 1, 3),
    )


def send_matrices(tables, spaces):
    me, even, inner = roles(spaces)
    hop = spaces // 4
    row = iota((256, LANES), 0)
    lane = iota((256, LANES), 1)
    line, place = line_lanes(row)
    out = []
    for edge in swap_edges(even, inner):
        offset = jnp.where(edge == 0, -1, jnp.where(edge == 1, hop, jnp.where(edge == 2, 1, -hop)))
        target = lax.rem(me - offset + spaces, spaces)
        k = tables[1, edge, target]
        r = tables[2, edge, target]
        turned = (r == 1) | (r == 2)
        want = jnp.where(turned, 63 - place, place)
        top = (line == k) & (lane == want)
        own = (line == lax.rem(edge + 2, 4)) & (lane - 64 == place)
        out.append(jnp.concatenate([jnp.where(top, 1.0, 0.0), jnp.where(own, 1.0, 0.0)], axis=0).astype(BF))
    return out


def by_edge(spaces, swaps):
    _, even, inner = roles(spaces)
    m1, m2, n1, n2 = [ref[...].astype(F32) for ref in swaps]
    order = (
        jnp.where(even, m2, m1),
        jnp.where(inner, n1, n2),
        jnp.where(even, m1, m2),
        jnp.where(inner, n2, n1),
    )
    low = iota((C, LANES), 1) < 64
    turned = [pltpu.roll(block, 64, 1) for block in order]
    lines = [jnp.where(low, order[e], turned[e + 1]) for e in (0, 2)]
    return jnp.concatenate(lines, axis=1).astype(BF), [block.astype(BF)[:, 0:64] for block in turned]


CHUNKS = 4


def send_kernel(spaces, tables_hbm, x_hbm, g_hbm, m1, m2, n1, n2, tables, x_ref, g_ref, table_sem, x_sem, g_sem):
    wide = PIX // CHUNKS
    fetch = pltpu.make_async_copy(tables_hbm, tables, table_sem)
    fetch.start()
    copies = []
    for part in range(CHUNKS):
        at = slice(part * wide, (part + 1) * wide)
        pair = [
            pltpu.make_async_copy(x_hbm.at[:, at], x_ref.at[:, at], x_sem.at[part]),
            pltpu.make_async_copy(g_hbm.at[:, at], g_ref.at[:, at], g_sem.at[part]),
        ]
        for copy in pair:
            copy.start()
        copies.append(pair)
    fetch.wait()
    matrices = send_matrices(tables, spaces)
    parts = [[], []]
    for part in range(CHUNKS):
        for field, ref in enumerate((x_ref, g_ref)):
            copies[part][field].wait()
            for t in range(part * TILES // CHUNKS, (part + 1) * TILES // CHUNKS):
                parts[field].append(edge_only(tile(ref, t).astype(F32)))
    both = [
        lines_from(parts[field], tile(ref, 0).astype(F32), tile(ref, TILES - 1).astype(F32))
        for field, ref in enumerate((x_ref, g_ref))
    ]
    both = jnp.concatenate(both, axis=1)
    for out, matrix in zip((m1, m2, n1, n2), matrices):
        out[...] = dot(both, matrix).astype(BF)


def weights_of(rules, where, corner):
    rule = rules[corner, where]
    first = jnp.where(rule == 0, 1.0, jnp.where(rule == 1, 0.0, 0.5)).astype(F32)
    return first, 1.0 - first


def user_matrix(tables, rules, me, spaces, edge, step):
    used = (edge + 2) % 4
    user = lax.rem(me + offsets_of(spaces)[edge] + spaces, spaces)
    k = tables[1, used, user]
    r = tables[2, used, user]
    turned = (r == 1) | (r == 2)
    q = iota((SIDE, 256), 0)
    line, place = line_lanes(iota((1, 256), 1))
    want = jnp.where(turned, 63 - place, place)
    mine = line == k
    value = jnp.where(mine & (q == want + 1 - step), 1.0, 0.0)
    which = used % 2
    corners = ((0, 1), (1, 3), (2, 3), (0, 2))[used]
    if step == 0:
        weight = weights_of(rules, user, corners[0])[which]
        value = value + jnp.where(mine & (want == 0) & (q == 0), weight, 0.0)
    if step == 2:
        weight = weights_of(rules, user, corners[1])[which]
        value = value + jnp.where(mine & (want == 63) & (q == 63), weight, 0.0)
    return value.astype(BF)


def halo_matrix(rules, me, step):
    row = iota((256, 256), 0)
    line, place = line_lanes(iota((1, 256), 1))
    at = place + step - 1
    inside = (at >= 0) & (at < 64)
    value = jnp.where(inside & (row == line * 64 + at), 1.0, 0.0)
    side = (line == 3) | (line == 1)
    left = line == 3
    if step != 1:
        if step == 0:
            active = side & (place == 0)
            row_a = jnp.where(left, 0, 63)
            row_b = jnp.where(left, 192, 64)
            pair = (0, 1)
        else:
            active = side & (place == 63)
            row_a = jnp.where(left, 128, 191)
            row_b = jnp.where(left, 255, 127)
            pair = (2, 3)
        fl, sl = weights_of(rules, me, pair[0])
        fr, sr = weights_of(rules, me, pair[1])
        value = value + jnp.where(active & (row == row_a), jnp.where(left, fl, fr), 0.0)
        value = value + jnp.where(active & (row == row_b), jnp.where(left, sl, sr), 0.0)
    return value.astype(BF)


def half_shift(dst, ref, before, after):
    low = iota((C, LANES), 1) < 64
    for t in range(TILES + 1):
        here = tile(ref, t) if t < TILES else after
        prev = tile(ref, t - 1) if t > 0 else before
        mixed = jnp.where(low, here.astype(F32), prev.astype(F32))
        dst[:, t * LANES : (t + 1) * LANES] = pltpu.roll(mixed, 64, 1).astype(BF)


def stack_of(half, ref, start, width):
    at = start * LANES
    size = width * LANES
    return jnp.concatenate(
        [half[:, at : at + size], ref[:, at : at + size], half[:, at + LANES : at + LANES + size]], axis=0
    )


def conv_tiles(weights, half, ref, columns, visit):
    at_left, at_right = lane_masks()
    for chunk in range(TILES // 2):
        taps = dot(weights, stack_of(half, ref, 2 * chunk, 2))
        for part in range(2):
            t = 2 * chunk + part
            lanes = slice(part * LANES, (part + 1) * LANES)
            side = 0.0 if columns is None else pltpu.roll(columns, (LANES - 2 * t) % LANES, 1)
            left = jnp.where(at_left, side, pltpu.roll(taps[0:C, lanes], 1, 1))
            right = jnp.where(at_right, side, pltpu.roll(taps[2 * C : 3 * C, lanes], LANES - 1, 1))
            visit(t, taps[C : 2 * C, lanes] + left + right)


def block_rows(taps, order):
    return jnp.concatenate([jnp.concatenate([taps[t] for t in row], axis=1) for row in order], axis=0)


def forward_form(taps):
    return block_rows(taps, [[b, 3 + b, 6 + b] for b in range(3)]).astype(BF)


def backward_form(taps):
    return block_rows(taps, [[8 - 3 * a - b for b in range(3)] for a in range(3)]).T.astype(BF)


def row_form(taps):
    return block_rows(taps, [[0, 1, 2], [6, 7, 8]]).astype(BF)


def return_form(taps):
    order = [[tap_of((edge + 2) % 4, step)] for edge in range(4) for step in range(3)]
    return block_rows(taps, order).T.astype(BF)


def float_taps(ref):
    return [ref[t].astype(F32) for t in range(9)]


def column(bias):
    row = jnp.broadcast_to(bias[...], (C, C))
    eye = iota((C, C), 0) == iota((C, C), 1)
    return jnp.broadcast_to(jnp.sum(jnp.where(eye, row, 0.0), axis=1, keepdims=True), (C, LANES))


def prepare_kernel(
    spaces, tables, rules, x_ref, g_ref, w1_ref, w2_ref,
    d_act, pre_in, x_side, route, halo, wf1, wr1, back2, half,
):
    me = lax.axis_index("space")
    taps1 = float_taps(w1_ref)
    taps2 = float_taps(w2_ref)
    wf1[...] = forward_form(taps1)
    wr1[...] = row_form(taps1)
    back2[...] = return_form(taps2)
    zero = jnp.zeros((C, LANES), BF)
    half_shift(half, g_ref, zero, zero)

    def keep(ref):
        def visit(t, value):
            ref[:, t * LANES : (t + 1) * LANES] = value

        return visit

    conv_tiles(backward_form(taps2), half, g_ref, None, keep(d_act))
    half_shift(half, x_ref, zero, zero)
    conv_tiles(wf1[...], half, x_ref, None, keep(pre_in))
    at_left, at_right = lane_masks()
    for t in range(TILES):
        at = slice(t * LANES, (t + 1) * LANES)
        x = tile(x_ref, t).astype(F32)
        x_side[0:C, at] = jnp.where(at_left, 0.0, pltpu.roll(x, 1, 1)).astype(BF)
        x_side[C : 2 * C, at] = jnp.where(at_right, 0.0, pltpu.roll(x, LANES - 1, 1)).astype(BF)
    for edge in range(4):
        for step in range(3):
            route[edge, :, step * 256 : (step + 1) * 256] = user_matrix(tables, rules, me, spaces, edge, step)
    for step in range(3):
        halo[:, step * 256 : (step + 1) * 256] = halo_matrix(rules, me, step)


def edge_terms(wf, wr, beside):
    stacked = jnp.concatenate([beside[:, s * 256 : (s + 1) * 256] for s in range(3)], axis=0)
    rows = dot(wr, stacked[:, 0:LANES])
    sides = dot(jnp.concatenate([wf[0:C], wf[2 * C : 3 * C]], axis=0), stacked[:, LANES:])
    lane = iota((C, LANES), 1)
    rows = jnp.where(lane < 64, rows[0:C], rows[C : 2 * C])
    return rows, jnp.where((lane & 1) == 0, sides[0:C], sides[C : 2 * C])


def add_edges(t, value, rows, sides):
    at_left, at_right = lane_masks()
    low = iota((C, LANES), 1) < 64
    value = value + jnp.where(at_left | at_right, pltpu.roll(sides, (LANES - 2 * t) % LANES, 1), 0.0)
    if t == 0:
        value = value + jnp.where(low, rows, 0.0)
    if t == TILES - 1:
        value = value + jnp.where(low, 0.0, rows)
    return value


def users_values(route, borders):
    parts = []
    for edge in range(4):
        moved = dot(borders[edge], route[edge]).astype(BF)
        parts += [moved[:, s * 256 : (s + 1) * 256] for s in range(3)]
    return jnp.concatenate(parts, axis=0)


def middle_kernel(
    spaces, tables, m1, m2, n1, n2, d_act, pre_in, route, halo, wf, wr, back, bias,
    act_ref, d_ref, p0, p1, p2, p3, beside_ref, users_ref, act_lines, d_lines,
):
    lines, borders = by_edge(spaces, (m1, m2, n1, n2))
    beside = dot(lines, halo[...]).astype(BF)
    beside_ref[...] = beside
    rows, sides = edge_terms(wf[...], wr[...], beside)
    users = users_values(route, borders)
    users_ref[...] = users
    line_grads = dot(back[...], users)
    d_rows = line_grads[:, 0:LANES]
    d_sides = line_grads[:, LANES : 2 * LANES]
    bias_now = column(bias)
    act_edges = []
    d_edges = []
    ends = {}
    for t in range(TILES):
        at = slice(t * LANES, (t + 1) * LANES)
        pre = add_edges(t, pre_in[:, at], rows, sides) + bias_now
        square = pre * pre
        inner = 0.7978845608028654 * pre * (1.0 + 0.044715 * square)
        wave = jnp.tanh(inner)
        cdf = 0.5 + 0.5 * wave
        slope = cdf + 0.5 * pre * (1.0 - wave * wave) * (0.7978845608028654 + 0.1070322243 * square)
        grad = add_edges(t, d_act[:, at], d_rows, d_sides)
        act = (pre * cdf).astype(BF)
        d_pre = (grad * slope).astype(BF)
        act_ref[:, at] = act
        d_ref[:, at] = d_pre
        act = act.astype(F32)
        d_pre = d_pre.astype(F32)
        act_edges.append(edge_only(act))
        d_edges.append(edge_only(d_pre))
        if t in (0, TILES - 1):
            ends[t] = (act, d_pre)
    act_l = lines_from(act_edges, ends[0][0], ends[TILES - 1][0])
    d_l = lines_from(d_edges, ends[0][1], ends[TILES - 1][1])
    act_lines[...] = act_l
    d_lines[...] = d_l
    both = jnp.concatenate([act_l, d_l], axis=1)
    for out, matrix in zip((p0, p1, p2, p3), send_matrices(tables, spaces)):
        out[...] = dot(both, matrix).astype(BF)


WIDE = 512
BIAS_AT = 9 * C


def grads_kernel(
    parts, x_ref, g_ref, act_ref, d_ref, x_side, beside, users, act_lines, d_lines,
    mine, other, half_a, half_d, held_one, held_two, near_one, near_two,
):
    zero = jnp.zeros((C, LANES), BF)
    half_shift(half_a, act_ref, zero, zero)
    half_shift(half_d, d_ref, zero, zero)
    width = 4
    at_left, at_right = lane_masks()
    one = jnp.zeros((3 * C, 3 * C), F32)
    two = jnp.zeros((3 * C, 3 * C), F32)
    ones = jnp.zeros((C, LANES), F32)
    twos = jnp.zeros((C, LANES), F32)
    for start in range(0, TILES, width):
        at = slice(start * LANES, (start + width) * LANES)
        g_tiles = [tile(g_ref, t).astype(F32) for t in range(start, start + width)]
        after = [jnp.where(at_right, 0.0, pltpu.roll(g, LANES - 1, 1)).astype(BF) for g in g_tiles]
        before = [jnp.where(at_left, 0.0, pltpu.roll(g, 1, 1)).astype(BF) for g in g_tiles]
        g_now = [jnp.concatenate(after, axis=1), g_ref[:, at], jnp.concatenate(before, axis=1)]
        g_now = jnp.concatenate(g_now, axis=0)
        x_now = jnp.concatenate([x_side[0:C, at], x_ref[:, at], x_side[C : 2 * C, at]], axis=0)
        two = two + dot_nt(g_now, stack_of(half_a, act_ref, start, width))
        one = one + dot_nt(stack_of(half_d, d_ref, start, width), x_now)
        for t in range(start, start + width):
            ones = ones + tile(d_ref, t).astype(F32)
            twos = twos + g_tiles[t - start]
    held_one[...] = one
    held_two[...] = two
    line, _ = line_lanes(iota((C, 256), 1))
    d_l = d_lines[...].astype(F32)
    d_by_edge = jnp.concatenate([jnp.where(line == e, d_l, 0.0) for e in range(4)], axis=0).astype(BF)
    near_one[...] = dot_nt(d_by_edge, jnp.concatenate([beside[:, s * 256 : (s + 1) * 256] for s in range(3)], axis=0))
    near_two[...] = dot_nt(users[...], act_lines[...])

    def block_one(a, b):
        value = held_one[(2 - a) * C : (3 - a) * C, b * C : (b + 1) * C]
        for edge in range(4):
            for step in range(3):
                if tap_of(edge, step) == 3 * a + b:
                    value = value + near_one[edge * C : (edge + 1) * C, step * C : (step + 1) * C]
        return value

    def block_two(a, b):
        value = held_two[b * C : (b + 1) * C, a * C : (a + 1) * C]
        for edge in range(4):
            for step in range(3):
                if tap_of(edge, step) == 3 * a + b:
                    at = ((edge + 2) % 4) * 3 + step
                    value = value + near_two[at * C : (at + 1) * C, :]
        return value

    def whole(block, bias):
        tail = jnp.broadcast_to(jnp.sum(bias, axis=1, keepdims=True), (C, WIDE - BIAS_AT))
        return jnp.concatenate([block(a, b) for a in range(3) for b in range(3)] + [tail], axis=1)

    first = whole(block_one, ones)
    second = whole(block_two, twos)
    even = (lax.axis_index("space") % 2) == 0
    keep = jnp.where(even, first, second)
    give = jnp.where(even, second, first)
    share = C // parts
    for part in range(parts):
        mine[part] = keep[part * share : (part + 1) * share]
        other[part] = give[part * share : (part + 1) * share]


def inner_kernel(g_ref, d_ref, w_ref, d_in, half):
    zero = jnp.zeros((C, LANES), BF)
    half_shift(half, d_ref, zero, zero)

    def visit(t, value):
        at = slice(t * LANES, (t + 1) * LANES)
        d_in[:, at] = value + g_ref[:, at].astype(F32)

    conv_tiles(backward_form(float_taps(w_ref)), half, d_ref, None, visit)


def output_kernel(spaces, x_ref, act_ref, m1, m2, n1, n2, halo, w_ref, bias, out, half):
    lines, _ = by_edge(spaces, (m1, m2, n1, n2))
    taps = float_taps(w_ref)
    wf = forward_form(taps)
    zero = jnp.zeros((C, LANES), BF)
    half_shift(half, act_ref, zero, zero)
    beside = dot(lines, halo[...]).astype(BF)
    rows, sides = edge_terms(wf, row_form(taps), beside)
    bias_now = column(bias)

    def visit(t, value):
        at = slice(t * LANES, (t + 1) * LANES)
        out[:, at] = (add_edges(t, value, rows, sides) + bias_now + x_ref[:, at].astype(F32)).astype(BF)

    conv_tiles(wf, half, act_ref, None, visit)


def grad_in_kernel(spaces, d_in, m1, m2, n1, n2, route, w_ref, out):
    _, borders = by_edge(spaces, (m1, m2, n1, n2))
    line_grads = dot(return_form(float_taps(w_ref)), users_values(route, borders))
    for t in range(TILES):
        at = slice(t * LANES, (t + 1) * LANES)
        out[:, at] = add_edges(t, d_in[:, at], line_grads[:, 0:LANES], line_grads[:, LANES : 2 * LANES]).astype(BF)


def unpack_kernel(share, own, got, grad_one, bias_one, grad_two, bias_two):
    even = (lax.axis_index("space") % 2) == 0
    first = jnp.where(even, own[...], got[...])
    second = jnp.where(even, got[...], own[...])
    eye = iota((share, LANES), 0) == iota((share, LANES), 1)
    for value, grad, bias in ((first, grad_one, bias_one), (second, grad_two, bias_two)):
        for tap in range(9):
            grad[tap] = value[:, tap * C : (tap + 1) * C]
        tail = jnp.broadcast_to(value[:, BIAS_AT : BIAS_AT + 1], (share, LANES))
        bias[...] = jnp.sum(jnp.where(eye, tail, 0.0), axis=0, keepdims=True)[:, 0:share]


def call(kernel, outs, specs, args, scratch=(), read=0, room=16 * 2**20):
    return pl.pallas_call(
        kernel,
        out_shape=[jax.ShapeDtypeStruct(shape, dtype) for shape, dtype in outs],
        in_specs=specs,
        out_specs=[VMEM] * len(outs),
        scratch_shapes=list(scratch),
        compiler_params=pltpu.CompilerParams(vmem_limit_bytes=room),
        cost_estimate=pl.CostEstimate(flops=0, bytes_accessed=read, transcendentals=0),
    )(*args)


HBM = pl.BlockSpec(memory_space=pltpu.HBM)


def exchange(blocks, spaces):
    hop = spaces // 4

    def first(i, step):
        return (i + step) % spaces if (i // step) % 2 == 0 else (i - step) % spaces

    def second(i, step):
        return (i - step) % spaces if (i // step) % 2 == 0 else (i + step) % spaces

    partner = (lambda i: first(i, 1), lambda i: second(i, 1), lambda i: first(i, hop), lambda i: second(i, hop))
    return [lax.ppermute(b, "space", [(i, to(i)) for i in range(spaces)]) for b, to in zip(blocks, partner)]


def swapped(block, mask, devices):
    return lax.ppermute(block, ("dp", "space"), [(i, i ^ mask) for i in range(devices)])


def total_over_chips(held, parts, spaces):
    devices = parts * spaces
    part_bits = [1 << bit for bit in reversed(range(parts.bit_length() - 1))]
    space_bits = [1 << bit for bit in range(1, spaces.bit_length() - 1)]
    rounds = [[(True, bit)] for bit in part_bits]
    for bit in space_bits:
        if len(rounds[-1]) == 1:
            rounds[-1].append((False, bit))
        elif len(rounds[0]) == 1:
            next(r for r in rounds if len(r) == 1).append((False, bit))
        else:
            rounds.append([(False, bit)])
    where = lax.axis_index("dp")
    for bits in rounds:
        keep = give = held.astype(BF)
        masks = []
        for is_part, bit in bits:
            masks.append(bit * spaces if is_part else bit)
            if is_part:
                upper = (where // bit) % 2 == 1
                low, high = keep[: keep.shape[0] // 2], keep[keep.shape[0] // 2 :]
                keep, give = jnp.where(upper, high, low), jnp.where(upper, low, high)
        split = bits[0][0]
        got = [swapped(give if split else keep, masks[0], devices)]
        if len(masks) == 2:
            got.append(swapped(keep, masks[1], devices))
            got.append(swapped(give if split else keep, masks[0] ^ masks[1], devices))
        terms = [value.astype(F32) for value in [keep] + got]
        held = terms[0] + terms[1]
        if len(masks) == 2:
            held = held + (terms[2] + terms[3])
    return held[0]


COST = 3_690_000


def on_device(inputs, cotangent, conv_one, bias_one, conv_two, bias_two, neighbours, corner_rule):
    parts = lax.axis_size("dp")
    spaces = lax.axis_size("space")
    share = C // parts
    x = inputs.reshape(C, PIX)
    g = cotangent.reshape(C, PIX)
    line = ((C, LANES), BF)
    image = ((C, PIX), BF)
    wide = ((C, PIX), F32)
    half = pltpu.VMEM((C, PIX + LANES), BF)
    tables = neighbours.transpose(2, 1, 0)
    rules = corner_rule.transpose(1, 0)

    sent = call(
        functools.partial(send_kernel, spaces), [line] * 4, [HBM, HBM, HBM], (tables, x, g),
        [pltpu.SMEM(tables.shape, jnp.int32), pltpu.VMEM((C, PIX), BF), pltpu.VMEM((C, PIX), BF),
         pltpu.SemaphoreType.DMA, pltpu.SemaphoreType.DMA((CHUNKS,)), pltpu.SemaphoreType.DMA((CHUNKS,))],
        read=COST * 2, room=66_900_000,
    )
    arrived = exchange(sent, spaces)
    square = ((3 * C, 3 * C), BF)
    rows = ((2 * C, 3 * C), BF)
    back = ((C, 12 * C), BF)
    d_act, pre_in, x_side, route, halo, wf1, wr1, back2 = call(
        functools.partial(prepare_kernel, spaces),
        [wide, wide, ((2 * C, PIX), BF), ((4, SIDE, 768), BF), ((256, 768), BF), square, rows, back],
        [SMEM, SMEM, VMEM, VMEM, VMEM, VMEM],
        (tables, rules, x, g, conv_one, conv_two), [half], read=COST * 3,
    )
    middle = call(
        functools.partial(middle_kernel, spaces),
        [image, image] + [line] * 4 + [((C, 768), BF), ((12 * C, 256), BF), ((C, 256), BF), ((C, 256), BF)],
        [SMEM] + [VMEM] * 12,
        (tables, *arrived, d_act, pre_in, route, halo, wf1, wr1, back2, bias_one.reshape(1, C)),
        read=COST * 9 // 4,
    )
    act, d_pre = middle[:2]
    beside, users, act_lines, d_lines = middle[6:]
    packed = ((parts, share, WIDE), F32)
    mine, other = call(
        functools.partial(grads_kernel, parts), [packed, packed], [VMEM] * 9,
        (x, g, act, d_pre, x_side, beside, users, act_lines, d_lines),
        [half, half, pltpu.VMEM((3 * C, 3 * C), F32), pltpu.VMEM((3 * C, 3 * C), F32),
         pltpu.VMEM((4 * C, 3 * C), F32), pltpu.VMEM((12 * C, C), F32)],
        read=COST * 5 // 4,
    )
    devices = parts * spaces
    held = mine + swapped(other, 1, devices)
    held, *blocks = lax.optimization_barrier((held, *middle[2:6]))
    again = exchange(blocks, spaces)
    own = total_over_chips(held, parts, spaces)
    (d_in,) = call(inner_kernel, [wide], [VMEM] * 3, (g, d_pre, conv_one), [half], read=COST)
    (output,) = call(
        functools.partial(output_kernel, spaces), [image], [VMEM] * 9,
        (x, act, *again, halo, conv_two, bias_two.reshape(1, C)), [half], read=COST * 3 // 2,
    )
    (grad_in,) = call(
        functools.partial(grad_in_kernel, spaces), [image], [VMEM] * 7, (d_in, *again, route, conv_one),
        read=COST * 7 // 4,
    )
    own, output, grad_in = lax.optimization_barrier((own, output, grad_in))
    got = swapped(own, 1, devices)
    taps = ((9, share, C), F32)
    bias = ((1, share), F32)
    grad_one, sum_one, grad_two, sum_two = call(
        functools.partial(unpack_kernel, share), [taps, bias, taps, bias], [VMEM] * 2, (own, got), read=10**5
    )
    shape = inputs.shape
    return (
        output.reshape(shape),
        grad_in.reshape(shape),
        grad_one,
        sum_one.reshape(share),
        grad_two,
        sum_two.reshape(share),
    )


def solution(mesh):
    tiles = P("dp", "space", None, None)
    return jax.shard_map(
        on_device,
        mesh=mesh,
        in_specs=(tiles, tiles, P(), P(), P(), P(), P(), P()),
        out_specs=(tiles, tiles, P(None, "dp", None), P("dp"), P(None, "dp", None), P("dp")),
        check_vma=False,
    )
```

```python
import functools

import jax
import jax.numpy as jnp
from jax import lax
from jax.experimental import pallas as pl
from jax.experimental.pallas import tpu as pltpu
from jax.sharding import PartitionSpec as P

BF = jnp.bfloat16
F32 = jnp.float32
C = 48
SIDE = 64
PIX = SIDE * SIDE
LANES = 128
TILES = PIX // LANES

VMEM = pl.BlockSpec(memory_space=pltpu.VMEM)


def tap_of(edge, step):
    return (step, 3 * step + 2, 6 + step, 3 * step)[edge]


def offsets_of(spaces):
    return (-1, spaces // 4, 1, -(spaces // 4))


def dot(a, b):
    return jnp.dot(a, b, preferred_element_type=F32)


def dot_nt(a, b):
    return lax.dot_general(a, b, (((1,), (1,)), ((), ())), preferred_element_type=F32)


def iota(shape, axis):
    return lax.broadcasted_iota(jnp.int32, shape, axis)


def line_lanes(lane):
    z = lane - 128
    even = (z & 1) == 0
    left = jnp.where(z < 64, z, z - 63)
    right = jnp.where(z < 63, z + 2, jnp.where(z < 127, z - 63, 1))
    line = jnp.where(lane < 64, 0, jnp.where(lane < 128, 2, jnp.where(even, 3, 1)))
    place = jnp.where(lane < 64, lane, jnp.where(lane < 128, lane - 64, jnp.where(even, left, right)))
    return line, place


def lane_masks():
    lane = iota((C, LANES), 1) & 63
    return lane == 0, lane == 63


def tile(ref, t):
    return ref[:, t * LANES : (t + 1) * LANES]


def lines_from(tiles, first, last):
    total = tiles[0]
    for t in range(1, TILES):
        total = total + pltpu.roll(tiles[t], 2 * t, 1)
    low = iota((C, LANES), 1) < 64
    rows = jnp.where(low, first, last)
    return jnp.concatenate([rows, total], axis=1).astype(BF)


def edge_only(values):
    at_left, at_right = lane_masks()
    return jnp.where(at_left | at_right, values, 0.0)


def roles(spaces):
    me = lax.axis_index("space")
    return me, (me % 2) == 0, ((me // (spaces // 4)) % 2) == 0


def swap_edges(even, inner):
    return (
        jnp.where(even, 0, 2),
        jnp.where(even, 2, 0),
        jnp.where(inner, 3, 1),
        jnp.where(inner, 1, 3),
    )


def send_matrices(tables, spaces):
    me, even, inner = roles(spaces)
    hop = spaces // 4
    row = iota((256, LANES), 0)
    lane = iota((256, LANES), 1)
    line, place = line_lanes(row)
    out = []
    for edge in swap_edges(even, inner):
        offset = jnp.where(edge == 0, -1, jnp.where(edge == 1, hop, jnp.where(edge == 2, 1, -hop)))
        target = lax.rem(me - offset + spaces, spaces)
        k = tables[1, edge, target]
        r = tables[2, edge, target]
        turned = (r == 1) | (r == 2)
        want = jnp.where(turned, 63 - place, place)
        top = (line == k) & (lane == want)
        own = (line == lax.rem(edge + 2, 4)) & (lane - 64 == place)
        out.append(jnp.concatenate([jnp.where(top, 1.0, 0.0), jnp.where(own, 1.0, 0.0)], axis=0).astype(BF))
    return out


def by_edge(spaces, swaps):
    _, even, inner = roles(spaces)
    m1, m2, n1, n2 = [ref[0:C].astype(F32) for ref in swaps]
    order = (
        jnp.where(even, m2, m1),
        jnp.where(inner, n1, n2),
        jnp.where(even, m1, m2),
        jnp.where(inner, n2, n1),
    )
    low = iota((C, LANES), 1) < 64
    turned = [pltpu.roll(block, 64, 1) for block in order]
    lines = [jnp.where(low, order[e], turned[e + 1]) for e in (0, 2)]
    return jnp.concatenate(lines, axis=1).astype(BF), [block.astype(BF)[:, 0:64] for block in turned]


CHUNKS = 4


def send_kernel(
    spaces, tables_hbm, x_hbm, g_hbm, m1, m2, n1, n2, x_ref, g_ref, tables, table_sem, x_sem, g_sem,
):
    wide = PIX // CHUNKS
    fetch = pltpu.make_async_copy(tables_hbm, tables, table_sem)
    fetch.start()
    copies = []
    for part in range(CHUNKS):
        at = slice(part * wide, (part + 1) * wide)
        pair = [
            pltpu.make_async_copy(x_hbm.at[:, at], x_ref.at[:, at], x_sem.at[part]),
            pltpu.make_async_copy(g_hbm.at[:, at], g_ref.at[:, at], g_sem.at[part]),
        ]
        for copy in pair:
            copy.start()
        copies.append(pair)
    fetch.wait()
    matrices = send_matrices(tables, spaces)
    parts = [[], []]
    for part in range(CHUNKS):
        for field, ref in enumerate((x_ref, g_ref)):
            copies[part][field].wait()
            for t in range(part * TILES // CHUNKS, (part + 1) * TILES // CHUNKS):
                parts[field].append(edge_only(tile(ref, t).astype(F32)))
    both = [
        lines_from(parts[field], tile(ref, 0).astype(F32), tile(ref, TILES - 1).astype(F32))
        for field, ref in enumerate((x_ref, g_ref))
    ]
    both = jnp.concatenate(both, axis=1)
    for out, matrix in zip((m1, m2, n1, n2), matrices):
        out[...] = dot(both, matrix).astype(BF)


def weights_of(rules, where, corner):
    rule = rules[corner, where]
    first = jnp.where(rule == 0, 1.0, jnp.where(rule == 1, 0.0, 0.5)).astype(F32)
    return first, 1.0 - first


def user_matrix(tables, rules, me, spaces, edge, step):
    used = (edge + 2) % 4
    user = lax.rem(me + offsets_of(spaces)[edge] + spaces, spaces)
    k = tables[1, used, user]
    r = tables[2, used, user]
    turned = (r == 1) | (r == 2)
    q = iota((SIDE, 256), 0)
    line, place = line_lanes(iota((1, 256), 1))
    want = jnp.where(turned, 63 - place, place)
    mine = line == k
    value = jnp.where(mine & (q == want + 1 - step), 1.0, 0.0)
    which = used % 2
    corners = ((0, 1), (1, 3), (2, 3), (0, 2))[used]
    if step == 0:
        weight = weights_of(rules, user, corners[0])[which]
        value = value + jnp.where(mine & (want == 0) & (q == 0), weight, 0.0)
    if step == 2:
        weight = weights_of(rules, user, corners[1])[which]
        value = value + jnp.where(mine & (want == 63) & (q == 63), weight, 0.0)
    return value.astype(BF)


def halo_matrix(rules, me, step):
    row = iota((256, LANES), 0)
    line, place = line_lanes(iota((1, LANES), 1) + LANES)
    at = place + step - 1
    inside = (at >= 0) & (at < 64)
    value = jnp.where(inside & (row == line * 64 + at), 1.0, 0.0)
    left = line == 3
    if step != 1:
        if step == 0:
            active = place == 0
            row_a = jnp.where(left, 0, 63)
            row_b = jnp.where(left, 192, 64)
            pair = (0, 1)
        else:
            active = place == 63
            row_a = jnp.where(left, 128, 191)
            row_b = jnp.where(left, 255, 127)
            pair = (2, 3)
        fl, sl = weights_of(rules, me, pair[0])
        fr, sr = weights_of(rules, me, pair[1])
        value = value + jnp.where(active & (row == row_a), jnp.where(left, fl, fr), 0.0)
        value = value + jnp.where(active & (row == row_b), jnp.where(left, sl, sr), 0.0)
    return value.astype(BF)


def beside_lines(lines, halo):
    columns = dot(lines, halo[...]).astype(BF)
    low = iota((C, LANES), 1) < 64
    at_left, at_right = lane_masks()
    upper = lines[:, 0:LANES].astype(F32)
    lower = lines[:, LANES:].astype(F32)
    rows = jnp.where(low, upper, pltpu.roll(lower, 64, 1))
    moved = (
        jnp.where(at_left, 0.0, pltpu.roll(rows, 1, 1)),
        rows,
        jnp.where(at_right, 0.0, pltpu.roll(rows, LANES - 1, 1)),
    )
    parts = [
        jnp.concatenate([moved[s].astype(BF), columns[:, s * LANES : (s + 1) * LANES]], axis=1) for s in range(3)
    ]
    return jnp.concatenate(parts, axis=0)


def half_shift(dst, ref, before, after):
    low = iota((C, LANES), 1) < 64
    for t in range(TILES + 1):
        here = tile(ref, t) if t < TILES else after
        prev = tile(ref, t - 1) if t > 0 else before
        mixed = jnp.where(low, here.astype(F32), prev.astype(F32))
        dst[:, t * LANES : (t + 1) * LANES] = pltpu.roll(mixed, 64, 1).astype(BF)


def stack_of(half, ref, start, width):
    at = start * LANES
    size = width * LANES
    return jnp.concatenate(
        [half[:, at : at + size], ref[:, at : at + size], half[:, at + LANES : at + LANES + size]], axis=0
    )


def conv_tiles(weights, half, ref, columns, visit):
    at_left, at_right = lane_masks()
    for chunk in range(TILES // 2):
        taps = dot(weights, stack_of(half, ref, 2 * chunk, 2))
        for part in range(2):
            t = 2 * chunk + part
            lanes = slice(part * LANES, (part + 1) * LANES)
            side = 0.0 if columns is None else pltpu.roll(columns, (LANES - 2 * t) % LANES, 1)
            left = jnp.where(at_left, side, pltpu.roll(taps[0:C, lanes], 1, 1))
            right = jnp.where(at_right, side, pltpu.roll(taps[2 * C : 3 * C, lanes], LANES - 1, 1))
            visit(t, taps[C : 2 * C, lanes] + left + right)


def block_rows(taps, order):
    return jnp.concatenate([jnp.concatenate([taps[t] for t in row], axis=1) for row in order], axis=0)


def forward_form(taps):
    return block_rows(taps, [[b, 3 + b, 6 + b] for b in range(3)]).astype(BF)


def backward_form(taps):
    return block_rows(taps, [[8 - 3 * a - b for b in range(3)] for a in range(3)]).T.astype(BF)


def row_form(taps):
    return block_rows(taps, [[0, 1, 2], [6, 7, 8]]).astype(BF)


def return_form(taps):
    order = [[tap_of((edge + 2) % 4, step)] for edge in range(4) for step in range(3)]
    return block_rows(taps, order).T.astype(BF)


def float_taps(ref):
    return [ref[t].astype(F32) for t in range(9)]


def column(bias):
    row = jnp.broadcast_to(bias[...], (C, C))
    eye = iota((C, C), 0) == iota((C, C), 1)
    return jnp.broadcast_to(jnp.sum(jnp.where(eye, row, 0.0), axis=1, keepdims=True), (C, LANES))


def prepare_kernel(
    spaces, tables_hbm, rules_hbm, x_ref, g_ref, w1_ref, w2_ref, b1_ref, b2_ref,
    d_act, pre_in, x_side, route, halo, w_edge, back2, w1_out, w2_out, b1_out, b2_out,
    half, tables, rules, table_sem,
):
    fetches = [
        pltpu.make_async_copy(tables_hbm, tables, table_sem.at[0]),
        pltpu.make_async_copy(rules_hbm, rules, table_sem.at[1]),
    ]
    for fetch in fetches:
        fetch.start()
    me = lax.axis_index("space")
    taps1 = float_taps(w1_ref)
    taps2 = float_taps(w2_ref)
    wf1 = forward_form(taps1)
    w_edge[0 : 2 * C] = row_form(taps1)
    w_edge[2 * C :] = jnp.concatenate([wf1[0:C], wf1[2 * C : 3 * C]], axis=0)
    back2[...] = return_form(taps2)
    w1_out[...] = w1_ref[...]
    w2_out[...] = w2_ref[...]
    b1_out[...] = column(b1_ref)
    b2_out[...] = column(b2_ref)
    zero = jnp.zeros((C, LANES), BF)
    half_shift(half, g_ref, zero, zero)

    def keep(ref):
        def visit(t, value):
            ref[:, t * LANES : (t + 1) * LANES] = value

        return visit

    conv_tiles(backward_form(taps2), half, g_ref, None, keep(d_act))
    half_shift(half, x_ref, zero, zero)
    conv_tiles(wf1, half, x_ref, None, keep(pre_in))
    at_left, at_right = lane_masks()
    for t in range(TILES):
        at = slice(t * LANES, (t + 1) * LANES)
        x = tile(x_ref, t).astype(F32)
        x_side[0:C, at] = jnp.where(at_left, 0.0, pltpu.roll(x, 1, 1)).astype(BF)
        x_side[C : 2 * C, at] = jnp.where(at_right, 0.0, pltpu.roll(x, LANES - 1, 1)).astype(BF)
    for fetch in fetches:
        fetch.wait()
    for edge in range(4):
        for step in range(3):
            route[edge, :, step * 256 : (step + 1) * 256] = user_matrix(tables, rules, me, spaces, edge, step)
    for step in range(3):
        halo[:, step * LANES : (step + 1) * LANES] = halo_matrix(rules, me, step)


def edge_terms(w_sides, w_rows, stacked):
    rows = dot(w_rows, stacked[:, 0:LANES])
    sides = dot(w_sides, stacked[:, LANES:])
    lane = iota((C, LANES), 1)
    rows = jnp.where(lane < 64, rows[0:C], rows[C : 2 * C])
    return rows, jnp.where((lane & 1) == 0, sides[0:C], sides[C : 2 * C])


def add_edges(t, value, rows, sides):
    at_left, at_right = lane_masks()
    low = iota((C, LANES), 1) < 64
    value = value + jnp.where(at_left | at_right, pltpu.roll(sides, (LANES - 2 * t) % LANES, 1), 0.0)
    if t == 0:
        value = value + jnp.where(low, rows, 0.0)
    if t == TILES - 1:
        value = value + jnp.where(low, 0.0, rows)
    return value


def users_values(route, borders):
    parts = []
    for edge in range(4):
        moved = dot(borders[edge], route[edge]).astype(BF)
        parts += [moved[:, s * 256 : (s + 1) * 256] for s in range(3)]
    return jnp.concatenate(parts, axis=0)


def middle_kernel(
    spaces, tables_hbm, m1, m2, n1, n2, d_act, pre_in, route, halo, w_edge, back, bias,
    act_ref, d_ref, p0, p1, p2, p3, beside_ref, users_ref, act_lines, d_lines, tables, table_sem,
):
    fetch = pltpu.make_async_copy(tables_hbm, tables, table_sem)
    fetch.start()
    lines, borders = by_edge(spaces, (m1, m2, n1, n2))
    beside = beside_lines(lines, halo)
    beside_ref[...] = beside
    rows, sides = edge_terms(w_edge[2 * C :], w_edge[0 : 2 * C], beside)
    users = users_values(route, borders)
    users_ref[...] = users
    line_grads = dot(back[...], users)
    d_rows = line_grads[:, 0:LANES]
    d_sides = line_grads[:, LANES : 2 * LANES]
    bias_now = bias[...]
    act_edges = []
    d_edges = []
    ends = {}
    for t in range(TILES):
        at = slice(t * LANES, (t + 1) * LANES)
        pre = add_edges(t, pre_in[:, at], rows, sides) + bias_now
        square = pre * pre
        inner = 0.7978845608028654 * pre * (1.0 + 0.044715 * square)
        wave = jnp.tanh(inner)
        cdf = 0.5 + 0.5 * wave
        slope = cdf + 0.5 * pre * (1.0 - wave * wave) * (0.7978845608028654 + 0.1070322243 * square)
        grad = add_edges(t, d_act[:, at], d_rows, d_sides)
        act = (pre * cdf).astype(BF)
        d_pre = (grad * slope).astype(BF)
        act_ref[:, at] = act
        d_ref[:, at] = d_pre
        act = act.astype(F32)
        d_pre = d_pre.astype(F32)
        act_edges.append(edge_only(act))
        d_edges.append(edge_only(d_pre))
        if t in (0, TILES - 1):
            ends[t] = (act, d_pre)
    act_l = lines_from(act_edges, ends[0][0], ends[TILES - 1][0])
    d_l = lines_from(d_edges, ends[0][1], ends[TILES - 1][1])
    act_lines[...] = act_l
    d_lines[...] = d_l
    both = jnp.concatenate([act_l, d_l], axis=1)
    fetch.wait()
    for out, matrix in zip((p0, p1, p2, p3), send_matrices(tables, spaces)):
        out[...] = dot(both, matrix).astype(BF)


WIDE = 512
BIAS_AT = 9 * C


def grads_kernel(
    parts, x_ref, g_ref, act_ref, d_ref, x_side, beside, users, act_lines, d_lines,
    mine, other, half_a, half_d, held_one, held_two, near_one, near_two,
):
    zero = jnp.zeros((C, LANES), BF)
    half_shift(half_a, act_ref, zero, zero)
    half_shift(half_d, d_ref, zero, zero)
    width = 4
    at_left, at_right = lane_masks()
    one = jnp.zeros((3 * C, 3 * C), F32)
    two = jnp.zeros((3 * C, 3 * C), F32)
    ones = jnp.zeros((C, LANES), F32)
    twos = jnp.zeros((C, LANES), F32)
    for start in range(0, TILES, width):
        at = slice(start * LANES, (start + width) * LANES)
        g_tiles = [tile(g_ref, t).astype(F32) for t in range(start, start + width)]
        after = [jnp.where(at_right, 0.0, pltpu.roll(g, LANES - 1, 1)).astype(BF) for g in g_tiles]
        before = [jnp.where(at_left, 0.0, pltpu.roll(g, 1, 1)).astype(BF) for g in g_tiles]
        g_now = [jnp.concatenate(after, axis=1), g_ref[:, at], jnp.concatenate(before, axis=1)]
        g_now = jnp.concatenate(g_now, axis=0)
        x_now = jnp.concatenate([x_side[0:C, at], x_ref[:, at], x_side[C : 2 * C, at]], axis=0)
        two = two + dot_nt(g_now, stack_of(half_a, act_ref, start, width))
        one = one + dot_nt(stack_of(half_d, d_ref, start, width), x_now)
        for t in range(start, start + width):
            ones = ones + tile(d_ref, t).astype(F32)
            twos = twos + g_tiles[t - start]
    held_one[...] = one
    held_two[...] = two
    line, _ = line_lanes(iota((C, 256), 1))
    d_l = d_lines[...].astype(F32)
    d_by_edge = jnp.concatenate([jnp.where(line == e, d_l, 0.0) for e in range(4)], axis=0).astype(BF)
    near_one[...] = dot_nt(d_by_edge, beside[...])
    near_two[...] = dot_nt(users[...], act_lines[...])

    def block_one(a, b):
        value = held_one[(2 - a) * C : (3 - a) * C, b * C : (b + 1) * C]
        for edge in range(4):
            for step in range(3):
                if tap_of(edge, step) == 3 * a + b:
                    value = value + near_one[edge * C : (edge + 1) * C, step * C : (step + 1) * C]
        return value

    def block_two(a, b):
        value = held_two[b * C : (b + 1) * C, a * C : (a + 1) * C]
        for edge in range(4):
            for step in range(3):
                if tap_of(edge, step) == 3 * a + b:
                    at = ((edge + 2) % 4) * 3 + step
                    value = value + near_two[at * C : (at + 1) * C, :]
        return value

    def whole(block, bias):
        tail = jnp.broadcast_to(jnp.sum(bias, axis=1, keepdims=True), (C, WIDE - BIAS_AT))
        return jnp.concatenate([block(a, b) for a in range(3) for b in range(3)] + [tail], axis=1)

    first = whole(block_one, ones)
    second = whole(block_two, twos)
    even = (lax.axis_index("space") % 2) == 0
    keep = jnp.where(even, first, second)
    give = jnp.where(even, second, first)
    share = C // parts
    for part in range(parts):
        at = slice(part * share, (part + 1) * share)
        mine[part] = jnp.concatenate([keep[at, j * LANES : (j + 1) * LANES] for j in range(WIDE // LANES)], axis=0)
        other[part] = jnp.concatenate([give[at, j * LANES : (j + 1) * LANES] for j in range(WIDE // LANES)], axis=0)


def inner_kernel(g_ref, d_ref, w_ref, d_in, half):
    zero = jnp.zeros((C, LANES), BF)
    half_shift(half, d_ref, zero, zero)

    def visit(t, value):
        at = slice(t * LANES, (t + 1) * LANES)
        d_in[:, at] = value + g_ref[:, at].astype(F32)

    conv_tiles(backward_form(float_taps(w_ref)), half, d_ref, None, visit)


def partial_kernel(x_ref, act_ref, w1_ref, w2_ref, bias, out, sides, back, half):
    taps = float_taps(w2_ref)
    wf = forward_form(taps)
    sides[0 : 2 * C] = row_form(taps)
    sides[2 * C :] = jnp.concatenate([wf[0:C], wf[2 * C : 3 * C]], axis=0)
    back[...] = return_form(float_taps(w1_ref))
    zero = jnp.zeros((C, LANES), BF)
    half_shift(half, act_ref, zero, zero)
    bias_now = bias[...]

    def visit(t, value):
        at = slice(t * LANES, (t + 1) * LANES)
        out[:, at] = value + bias_now + x_ref[:, at].astype(F32)

    conv_tiles(wf, half, act_ref, None, visit)


def finish_kernel(spaces, partial, d_in, m1, m2, n1, n2, halo, route, sides_ref, back, out, grad_in):
    lines, borders = by_edge(spaces, (m1, m2, n1, n2))
    rows, sides = edge_terms(sides_ref[2 * C :], sides_ref[0 : 2 * C], beside_lines(lines, halo))
    line_grads = dot(back[...], users_values(route, borders))
    for t in range(TILES):
        at = slice(t * LANES, (t + 1) * LANES)
        out[:, at] = add_edges(t, partial[:, at], rows, sides).astype(BF)
        grad_in[:, at] = add_edges(t, d_in[:, at], line_grads[:, 0:LANES], line_grads[:, LANES : 2 * LANES]).astype(BF)


def unpack_kernel(share, own, got, grad_one, bias_one, grad_two, bias_two):
    even = (lax.axis_index("space") % 2) == 0
    one = jnp.where(even, own[...], got[...])
    two = jnp.where(even, got[...], own[...])
    first, second = [
        jnp.concatenate([value[j * share : (j + 1) * share] for j in range(WIDE // LANES)], axis=1)
        for value in (one, two)
    ]
    eye = iota((share, LANES), 0) == iota((share, LANES), 1)
    for value, grad, bias in ((first, grad_one, bias_one), (second, grad_two, bias_two)):
        for tap in range(9):
            grad[tap] = value[:, tap * C : (tap + 1) * C]
        tail = jnp.broadcast_to(value[:, BIAS_AT : BIAS_AT + 1], (share, LANES))
        bias[...] = jnp.sum(jnp.where(eye, tail, 0.0), axis=0, keepdims=True)[:, 0:share]


def call(kernel, outs, specs, args, scratch=(), read=0, room=16 * 2**20):
    return pl.pallas_call(
        kernel,
        out_shape=[jax.ShapeDtypeStruct(shape, dtype) for shape, dtype in outs],
        in_specs=specs,
        out_specs=[VMEM] * len(outs),
        scratch_shapes=list(scratch),
        compiler_params=pltpu.CompilerParams(vmem_limit_bytes=room),
        cost_estimate=pl.CostEstimate(flops=0, bytes_accessed=read, transcendentals=0),
    )(*args)


HBM = pl.BlockSpec(memory_space=pltpu.HBM)


def in_hbm(value):
    return pltpu.with_memory_space_constraint(value, pltpu.HBM)


def swapped(block, mask, devices):
    return lax.ppermute(block, ("dp", "space"), [(i, i ^ mask) for i in range(devices)])


def swap_along(blocks, spaces, more=1):
    def second(i):
        return (i - 1) % spaces if i % 2 == 0 else (i + 1) % spaces

    return [
        lax.ppermute(blocks[0], "space", [(i, i ^ 1) for i in range(spaces)]),
        lax.ppermute(jnp.concatenate([blocks[1]] * more, axis=0) if more > 1 else blocks[1], "space", [(i, second(i)) for i in range(spaces)]),
    ]


def swap_across(blocks, spaces, devices):
    hop = spaces // 4
    return [swapped(blocks[0], hop, devices), swapped(blocks[1], hop ^ 2 * hop, devices)]


def first_rounds(parts, spaces):
    rounds = [[(True, 1 << bit)] for bit in reversed(range(parts.bit_length() - 1))]
    bit = 2
    while bit < spaces // 4:
        single = [r for r in rounds if len(r) == 1]
        if single:
            single[0].append((False, bit))
        else:
            rounds.append([(False, bit)])
        bit *= 2
    return rounds


def total_of(a, b, c, d):
    return (a.astype(F32) + b.astype(F32)) + (c.astype(F32) + d.astype(F32))


def last_round(held, blocks, spaces, devices):
    hop = spaces // 4
    held = held.astype(BF)
    joined = [jnp.concatenate([block, held], axis=0) for block in blocks]
    near, far = swap_across(joined, spaces, devices)
    opposite = swapped(held, 2 * hop, devices)
    return near, far, total_of(held, near[C:], opposite, far[C:])


def reduced(held, bits, devices, spaces, beside):
    where = lax.axis_index("dp")
    keep = give = held.astype(BF)
    masks = []
    for is_part, bit in bits:
        masks.append(bit * spaces if is_part else bit)
        if is_part:
            upper = (where // bit) % 2 == 1
            low, high = keep[: keep.shape[0] // 2], keep[keep.shape[0] // 2 :]
            keep, give = jnp.where(upper, high, low), jnp.where(upper, low, high)
    first = swapped(give, masks[0], devices)
    kept, *beside = lax.optimization_barrier((keep, *beside))
    if len(masks) == 1:
        return kept.astype(F32) + first.astype(F32), beside
    return total_of(kept, first, swapped(keep, masks[1], devices), swapped(give, masks[0] ^ masks[1], devices)), beside


COST = 3_690_000


def on_device(inputs, cotangent, conv_one, bias_one, conv_two, bias_two, neighbours, corner_rule):
    parts = lax.axis_size("dp")
    spaces = lax.axis_size("space")
    share = C // parts
    x = inputs.reshape(C, PIX)
    g = cotangent.reshape(C, PIX)
    line = ((C, LANES), BF)
    image = ((C, PIX), BF)
    wide = ((C, PIX), F32)
    half = pltpu.VMEM((C, PIX + LANES), BF)
    tables = neighbours.transpose(2, 1, 0)
    rules = corner_rule.transpose(1, 0)

    weights = (conv_one.shape, BF)
    bias = ((C, LANES), F32)
    *sent, x_near, g_near = call(
        functools.partial(send_kernel, spaces), [line] * 4 + [image, image], [HBM] * 3, (in_hbm(tables), in_hbm(x), in_hbm(g)),
        [pltpu.SMEM(tables.shape, jnp.int32), pltpu.SemaphoreType.DMA, pltpu.SemaphoreType.DMA((CHUNKS,)),
         pltpu.SemaphoreType.DMA((CHUNKS,))],
        read=COST * 2,
    )
    devices = parts * spaces
    arrived = swap_along(sent[:2], spaces, 4) + swap_across(sent[2:], spaces, devices)
    edges = ((4 * C, 3 * C), BF)
    back = ((C, 12 * C), BF)
    d_act, pre_in, x_side, route, halo, w_edge, back2, w_one, w_two, b_one, b_two = call(
        functools.partial(prepare_kernel, spaces),
        [wide, wide, ((2 * C, PIX), BF), ((4, SIDE, 768), BF), ((256, 384), BF), edges, back,
         weights, weights, bias, bias],
        [HBM, HBM] + [VMEM] * 6,
        (in_hbm(tables), in_hbm(rules), x_near, g_near, conv_one, conv_two, bias_one.reshape(1, C), bias_two.reshape(1, C)),
        [half, pltpu.SMEM(tables.shape, jnp.int32), pltpu.SMEM(rules.shape, jnp.int32), pltpu.SemaphoreType.DMA((2,))],
        read=COST * 3,
    )
    middle = call(
        functools.partial(middle_kernel, spaces),
        [image, image] + [line] * 4 + [((3 * C, 256), BF), ((12 * C, 256), BF), ((C, 256), BF), ((C, 256), BF)],
        [HBM] + [VMEM] * 11,
        (in_hbm(tables), *arrived, d_act, pre_in, route, halo, w_edge, back2, b_one),
        [pltpu.SMEM(tables.shape, jnp.int32), pltpu.SemaphoreType.DMA],
        read=COST * 9 // 4,
    )
    act, d_pre = middle[:2]
    beside, users, act_lines, d_lines = middle[6:]
    packed = ((parts, share * WIDE // LANES, LANES), F32)
    mine, other = call(
        functools.partial(grads_kernel, parts), [packed, packed], [VMEM] * 9,
        (x, g, act, d_pre, x_side, beside, users, act_lines, d_lines),
        [half, half, pltpu.VMEM((3 * C, 3 * C), F32), pltpu.VMEM((3 * C, 3 * C), F32),
         pltpu.VMEM((4 * C, 3 * C), F32), pltpu.VMEM((12 * C, C), F32)],
        read=COST * 5 // 4,
    )
    (d_in,) = call(inner_kernel, [wide], [VMEM] * 3, (g, d_pre, w_one), [half], read=COST)
    partial, edges_two, back_one = call(
        partial_kernel, [wide, edges, back], [VMEM] * 5, (x, act, w_one, w_two, b_two), [half], read=COST * 3 // 2
    )
    held = mine + swapped(other, 1, devices)
    held, d_in, *blocks = lax.optimization_barrier((held, d_in, *middle[2:6]))
    again = swap_along(blocks[:2], spaces, 4)
    for bits in first_rounds(parts, spaces):
        held, again = reduced(held, bits, devices, spaces, again)
    held, partial = lax.optimization_barrier((held, partial))
    near, far, own = last_round(held[0], blocks[2:], spaces, devices)
    got = swapped(own, 1, devices)
    output, grad_in = call(
        functools.partial(finish_kernel, spaces), [image, image], [VMEM] * 10,
        (partial, d_in, *again, near, far, halo, route, edges_two, back_one), read=COST * 3 // 2,
    )
    taps = ((9, share, C), F32)
    bias = ((1, share), F32)
    grad_one, sum_one, grad_two, sum_two = call(
        functools.partial(unpack_kernel, share), [taps, bias, taps, bias], [VMEM] * 2, (own, got), read=10**5
    )
    shape = inputs.shape
    return (
        output.reshape(shape),
        grad_in.reshape(shape),
        grad_one,
        sum_one.reshape(share),
        grad_two,
        sum_two.reshape(share),
    )


def solution(mesh):
    tiles = P("dp", "space", None, None)
    return jax.shard_map(
        on_device,
        mesh=mesh,
        in_specs=(tiles, tiles, P(), P(), P(), P(), P(), P()),
        out_specs=(tiles, tiles, P(None, "dp", None), P("dp"), P(None, "dp", None), P("dp")),
        check_vma=False,
    )
```

```python
import functools

import jax
import jax.numpy as jnp
from jax import lax
from jax.experimental import pallas as pl
from jax.experimental.pallas import tpu as pltpu
from jax.sharding import PartitionSpec as P

BF = jnp.bfloat16
F32 = jnp.float32
C = 48
SIDE = 64
PIX = SIDE * SIDE
LANES = 128
TILES = PIX // LANES

VMEM = pl.BlockSpec(memory_space=pltpu.VMEM)


def tap_of(edge, step):
    return (step, 3 * step + 2, 6 + step, 3 * step)[edge]


def offsets_of(spaces):
    return (-1, spaces // 4, 1, -(spaces // 4))


def dot(a, b):
    return jnp.dot(a, b, preferred_element_type=F32)


def dot_nt(a, b):
    return lax.dot_general(a, b, (((1,), (1,)), ((), ())), preferred_element_type=F32)


def iota(shape, axis):
    return lax.broadcasted_iota(jnp.int32, shape, axis)


def line_lanes(lane):
    z = lane - 128
    even = (z & 1) == 0
    left = jnp.where(z < 64, z, z - 63)
    right = jnp.where(z < 63, z + 2, jnp.where(z < 127, z - 63, 1))
    line = jnp.where(lane < 64, 0, jnp.where(lane < 128, 2, jnp.where(even, 3, 1)))
    place = jnp.where(lane < 64, lane, jnp.where(lane < 128, lane - 64, jnp.where(even, left, right)))
    return line, place


def lane_masks():
    lane = iota((C, LANES), 1) & 63
    return lane == 0, lane == 63


def tile(ref, t):
    return ref[:, t * LANES : (t + 1) * LANES]


def lines_from(tiles, first, last):
    total = tiles[0]
    for t in range(1, TILES):
        total = total + pltpu.roll(tiles[t], 2 * t, 1)
    low = iota((C, LANES), 1) < 64
    rows = jnp.where(low, first, last)
    return jnp.concatenate([rows, total], axis=1)


def edge_only(values):
    at_left, at_right = lane_masks()
    return jnp.where(at_left | at_right, values, jnp.zeros_like(values))


def roles(spaces):
    me = lax.axis_index("space")
    return me, (me % 2) == 0, ((me // (spaces // 4)) % 2) == 0


def swap_edges(even, inner):
    return (
        jnp.where(even, 0, 2),
        jnp.where(even, 2, 0),
        jnp.where(inner, 3, 1),
        jnp.where(inner, 1, 3),
    )


def send_choice(tables, spaces):
    me, even, inner = roles(spaces)
    hop = spaces // 4
    line, place = line_lanes(iota((256, 1), 0))
    lane = iota((1, LANES), 1)
    low = lane < 64
    spot = lane & 63
    chosen = []
    for edge in swap_edges(even, inner):
        offset = jnp.where(edge == 0, -1, jnp.where(edge == 1, hop, jnp.where(edge == 2, 1, -hop)))
        target = lax.rem(me - offset + spaces, spaces)
        k = tables[1, edge, target]
        r = tables[2, edge, target]
        turned = (r == 1) | (r == 2)
        wanted = jnp.where(low, k, lax.rem(edge + 2, 4)) * 64 + jnp.where(low & turned, 63 - spot, spot)
        chosen.append(jnp.where(line * 64 + place == wanted, 1.0, 0.0).astype(BF))
    return jnp.concatenate(chosen, axis=1)


def send_blocks(choice, field, border):
    moved = dot(jnp.concatenate([field, border], axis=0), choice)
    blocks = []
    for swap in range(4):
        at = slice(swap * LANES, (swap + 1) * LANES)
        blocks.append(jnp.where(iota((C, LANES), 1) < 64, moved[0:C, at], moved[C : 2 * C, at]).astype(BF))
    return blocks


def by_edge(spaces, swaps):
    _, even, inner = roles(spaces)
    m1, m2, n1, n2 = [ref[0:C] for ref in swaps]
    order = (
        jnp.where(even, m2, m1),
        jnp.where(inner, n1, n2),
        jnp.where(even, m1, m2),
        jnp.where(inner, n2, n1),
    )
    low = iota((C, LANES), 1) < 64
    turned = [pltpu.roll(block, 64, 1) for block in order]
    lines = [jnp.where(low, order[e], turned[e + 1]) for e in (0, 2)]
    return jnp.concatenate(lines, axis=1), [block[:, 0:64] for block in turned]


CHUNKS = 4


def send_kernel(
    spaces, tables_hbm, x_hbm, g_hbm, m1, m2, n1, n2, x_ref, g_ref, tables, table_sem, x_sem, g_sem,
):
    wide = PIX // CHUNKS
    fetch = pltpu.make_async_copy(tables_hbm, tables, table_sem)
    fetch.start()
    copies = []
    for part in range(CHUNKS):
        at = slice(part * wide, (part + 1) * wide)
        pair = [
            pltpu.make_async_copy(x_hbm.at[:, at], x_ref.at[:, at], x_sem.at[part]),
            pltpu.make_async_copy(g_hbm.at[:, at], g_ref.at[:, at], g_sem.at[part]),
        ]
        for copy in pair:
            copy.start()
        copies.append(pair)
    fetch.wait()
    choice = send_choice(tables, spaces)
    parts = [[], []]
    for part in range(CHUNKS):
        for field, ref in enumerate((x_ref, g_ref)):
            copies[part][field].wait()
            for t in range(part * TILES // CHUNKS, (part + 1) * TILES // CHUNKS):
                parts[field].append(edge_only(tile(ref, t)))
    both = [
        lines_from(parts[field], tile(ref, 0), tile(ref, TILES - 1))
        for field, ref in enumerate((x_ref, g_ref))
    ]
    for out, block in zip((m1, m2, n1, n2), send_blocks(choice, *both)):
        out[...] = block


def weights_of(rules, where, corner):
    rule = rules[corner, where]
    first = jnp.where(rule == 0, 1.0, jnp.where(rule == 1, 0.0, 0.5)).astype(F32)
    return first, 1.0 - first


def user_matrix(tables, rules, me, spaces, edge, step):
    used = (edge + 2) % 4
    user = lax.rem(me + offsets_of(spaces)[edge] + spaces, spaces)
    k = tables[1, used, user]
    r = tables[2, used, user]
    turned = (r == 1) | (r == 2)
    q = iota((SIDE, 256), 0)
    line, place = line_lanes(iota((1, 256), 1))
    want = jnp.where(turned, 63 - place, place)
    mine = line == k
    value = jnp.where(mine & (q == want + 1 - step), 1.0, 0.0)
    which = used % 2
    corners = ((0, 1), (1, 3), (2, 3), (0, 2))[used]
    if step == 0:
        weight = weights_of(rules, user, corners[0])[which]
        value = value + jnp.where(mine & (want == 0) & (q == 0), weight, 0.0)
    if step == 2:
        weight = weights_of(rules, user, corners[1])[which]
        value = value + jnp.where(mine & (want == 63) & (q == 63), weight, 0.0)
    return value.astype(BF)


def halo_matrix(rules, me, step):
    row = iota((256, LANES), 0)
    line, place = line_lanes(iota((1, LANES), 1) + LANES)
    at = place + step - 1
    inside = (at >= 0) & (at < 64)
    value = jnp.where(inside & (row == line * 64 + at), 1.0, 0.0)
    left = line == 3
    if step != 1:
        if step == 0:
            active = place == 0
            row_a = jnp.where(left, 0, 63)
            row_b = jnp.where(left, 192, 64)
            pair = (0, 1)
        else:
            active = place == 63
            row_a = jnp.where(left, 128, 191)
            row_b = jnp.where(left, 255, 127)
            pair = (2, 3)
        fl, sl = weights_of(rules, me, pair[0])
        fr, sr = weights_of(rules, me, pair[1])
        value = value + jnp.where(active & (row == row_a), jnp.where(left, fl, fr), 0.0)
        value = value + jnp.where(active & (row == row_b), jnp.where(left, sl, sr), 0.0)
    return value.astype(BF)


def beside_lines(lines, halo):
    columns = dot(lines, halo[...]).astype(BF)
    low = iota((C, LANES), 1) < 64
    at_left, at_right = lane_masks()
    rows = jnp.where(low, lines[:, 0:LANES], pltpu.roll(lines[:, LANES:], 64, 1))
    none = jnp.zeros_like(rows)
    moved = (
        jnp.where(at_left, none, pltpu.roll(rows, 1, 1)),
        rows,
        jnp.where(at_right, none, pltpu.roll(rows, LANES - 1, 1)),
    )
    parts = [
        jnp.concatenate([moved[s], columns[:, s * LANES : (s + 1) * LANES]], axis=1) for s in range(3)
    ]
    return jnp.concatenate(parts, axis=0)


def half_shift(dst, ref, before, after):
    low = iota((C, LANES), 1) < 64
    for t in range(TILES + 1):
        here = tile(ref, t) if t < TILES else after
        prev = tile(ref, t - 1) if t > 0 else before
        mixed = jnp.where(low, here.astype(F32), prev.astype(F32))
        dst[:, t * LANES : (t + 1) * LANES] = pltpu.roll(mixed, 64, 1).astype(BF)


def stack_of(half, ref, start, width):
    at = start * LANES
    size = width * LANES
    return jnp.concatenate(
        [half[:, at : at + size], ref[:, at : at + size], half[:, at + LANES : at + LANES + size]], axis=0
    )


def conv_tiles(weights, half, ref, columns, visit):
    at_left, at_right = lane_masks()
    for chunk in range(TILES // 2):
        taps = dot(weights, stack_of(half, ref, 2 * chunk, 2))
        for part in range(2):
            t = 2 * chunk + part
            lanes = slice(part * LANES, (part + 1) * LANES)
            side = 0.0 if columns is None else pltpu.roll(columns, (LANES - 2 * t) % LANES, 1)
            left = jnp.where(at_left, side, pltpu.roll(taps[0:C, lanes], 1, 1))
            right = jnp.where(at_right, side, pltpu.roll(taps[2 * C : 3 * C, lanes], LANES - 1, 1))
            visit(t, taps[C : 2 * C, lanes] + left + right)


def block_rows(taps, order):
    return jnp.concatenate([jnp.concatenate([taps[t] for t in row], axis=1) for row in order], axis=0)


def forward_form(taps):
    return block_rows(taps, [[b, 3 + b, 6 + b] for b in range(3)]).astype(BF)


def backward_form(taps):
    return block_rows(taps, [[8 - 3 * a - b for b in range(3)] for a in range(3)]).T.astype(BF)


def row_form(taps):
    return block_rows(taps, [[0, 1, 2], [6, 7, 8]]).astype(BF)


def return_form(taps):
    order = [[tap_of((edge + 2) % 4, step)] for edge in range(4) for step in range(3)]
    return block_rows(taps, order).T.astype(BF)


def float_taps(ref):
    return [ref[t].astype(F32) for t in range(9)]


def column(bias):
    row = jnp.broadcast_to(bias[...], (C, C))
    eye = iota((C, C), 0) == iota((C, C), 1)
    return jnp.broadcast_to(jnp.sum(jnp.where(eye, row, 0.0), axis=1, keepdims=True), (C, LANES))


def prepare_kernel(
    spaces, tables_hbm, rules_hbm, x_ref, g_ref, w1_ref, w2_ref, b1_ref, b2_ref,
    d_act, pre_in, x_side, route, halo, w_edge, back2, w1_out, w2_out, b1_out, b2_out,
    half, tables, rules, table_sem,
):
    fetches = [
        pltpu.make_async_copy(tables_hbm, tables, table_sem.at[0]),
        pltpu.make_async_copy(rules_hbm, rules, table_sem.at[1]),
    ]
    for fetch in fetches:
        fetch.start()
    me = lax.axis_index("space")
    taps1 = float_taps(w1_ref)
    taps2 = float_taps(w2_ref)
    wf1 = forward_form(taps1)
    w_edge[0 : 2 * C] = row_form(taps1)
    w_edge[2 * C :] = jnp.concatenate([wf1[0:C], wf1[2 * C : 3 * C]], axis=0)
    back2[...] = return_form(taps2)
    w1_out[...] = w1_ref[...]
    w2_out[...] = w2_ref[...]
    b1_out[...] = column(b1_ref)
    b2_out[...] = column(b2_ref)
    zero = jnp.zeros((C, LANES), BF)
    half_shift(half, g_ref, zero, zero)

    def keep(ref):
        def visit(t, value):
            ref[:, t * LANES : (t + 1) * LANES] = value

        return visit

    conv_tiles(backward_form(taps2), half, g_ref, None, keep(d_act))
    half_shift(half, x_ref, zero, zero)
    conv_tiles(wf1, half, x_ref, None, keep(pre_in))
    at_left, at_right = lane_masks()
    for t in range(TILES):
        at = slice(t * LANES, (t + 1) * LANES)
        x = tile(x_ref, t).astype(F32)
        x_side[0:C, at] = jnp.where(at_left, 0.0, pltpu.roll(x, 1, 1)).astype(BF)
        x_side[C : 2 * C, at] = jnp.where(at_right, 0.0, pltpu.roll(x, LANES - 1, 1)).astype(BF)
    for fetch in fetches:
        fetch.wait()
    for edge in range(4):
        for step in range(3):
            route[edge, :, step * 256 : (step + 1) * 256] = user_matrix(tables, rules, me, spaces, edge, step)
    for step in range(3):
        halo[:, step * LANES : (step + 1) * LANES] = halo_matrix(rules, me, step)


def edge_terms(w_sides, w_rows, stacked):
    rows = dot(w_rows, stacked[:, 0:LANES])
    sides = dot(w_sides, stacked[:, LANES:])
    lane = iota((C, LANES), 1)
    rows = jnp.where(lane < 64, rows[0:C], rows[C : 2 * C])
    return rows, jnp.where((lane & 1) == 0, sides[0:C], sides[C : 2 * C])


def add_edges(t, value, rows, sides):
    at_left, at_right = lane_masks()
    low = iota((C, LANES), 1) < 64
    value = value + jnp.where(at_left | at_right, pltpu.roll(sides, (LANES - 2 * t) % LANES, 1), 0.0)
    if t == 0:
        value = value + jnp.where(low, rows, 0.0)
    if t == TILES - 1:
        value = value + jnp.where(low, 0.0, rows)
    return value


def users_values(route, borders):
    parts = []
    for edge in range(4):
        moved = dot(borders[edge], route[edge]).astype(BF)
        parts += [moved[:, s * 256 : (s + 1) * 256] for s in range(3)]
    return jnp.concatenate(parts, axis=0)


def middle_kernel(
    spaces, tables_hbm, m1, m2, n1, n2, d_act, pre_in, route, halo, w_edge, back, bias,
    act_ref, d_ref, p0, p1, p2, p3, beside_ref, users_ref, act_lines, d_lines, tables, table_sem,
):
    fetch = pltpu.make_async_copy(tables_hbm, tables, table_sem)
    fetch.start()
    lines, borders = by_edge(spaces, (m1, m2, n1, n2))
    beside = beside_lines(lines, halo)
    beside_ref[...] = beside
    rows, sides = edge_terms(w_edge[2 * C :], w_edge[0 : 2 * C], beside)
    users = users_values(route, borders)
    users_ref[...] = users
    line_grads = dot(back[...], users)
    d_rows = line_grads[:, 0:LANES]
    d_sides = line_grads[:, LANES : 2 * LANES]
    bias_now = bias[...]
    act_edges = []
    d_edges = []
    ends = {}
    for t in range(TILES):
        at = slice(t * LANES, (t + 1) * LANES)
        pre = add_edges(t, pre_in[:, at], rows, sides) + bias_now
        square = pre * pre
        inner = 0.7978845608028654 * pre * (1.0 + 0.044715 * square)
        wave = jnp.tanh(inner)
        cdf = 0.5 + 0.5 * wave
        slope = cdf + 0.5 * pre * (1.0 - wave * wave) * (0.7978845608028654 + 0.1070322243 * square)
        grad = add_edges(t, d_act[:, at], d_rows, d_sides)
        act = (pre * cdf).astype(BF)
        d_pre = (grad * slope).astype(BF)
        act_ref[:, at] = act
        d_ref[:, at] = d_pre
        act_edges.append(edge_only(act))
        d_edges.append(edge_only(d_pre))
        if t in (0, TILES - 1):
            ends[t] = (act, d_pre)
    act_l = lines_from(act_edges, ends[0][0], ends[TILES - 1][0])
    d_l = lines_from(d_edges, ends[0][1], ends[TILES - 1][1])
    act_lines[...] = act_l
    d_lines[...] = d_l
    fetch.wait()
    for out, block in zip((p0, p1, p2, p3), send_blocks(send_choice(tables, spaces), act_l, d_l)):
        out[...] = block


WIDE = 512
BIAS_AT = 9 * C


def grads_kernel(
    parts, x_ref, g_ref, act_ref, d_ref, x_side, beside, users, act_lines, d_lines,
    mine, other, half_a, half_d, held_one, held_two, near_one, near_two,
):
    zero = jnp.zeros((C, LANES), BF)
    half_shift(half_a, act_ref, zero, zero)
    half_shift(half_d, d_ref, zero, zero)
    width = 4
    at_left, at_right = lane_masks()
    one = jnp.zeros((3 * C, 3 * C), F32)
    two = jnp.zeros((3 * C, 3 * C), F32)
    ones = jnp.zeros((C, LANES), F32)
    twos = jnp.zeros((C, LANES), F32)
    for start in range(0, TILES, width):
        at = slice(start * LANES, (start + width) * LANES)
        g_tiles = [tile(g_ref, t) for t in range(start, start + width)]
        after = [jnp.where(at_right, zero, pltpu.roll(g, LANES - 1, 1)) for g in g_tiles]
        before = [jnp.where(at_left, zero, pltpu.roll(g, 1, 1)) for g in g_tiles]
        g_now = [jnp.concatenate(after, axis=1), g_ref[:, at], jnp.concatenate(before, axis=1)]
        g_now = jnp.concatenate(g_now, axis=0)
        x_now = jnp.concatenate([x_side[0:C, at], x_ref[:, at], x_side[C : 2 * C, at]], axis=0)
        two = two + dot_nt(g_now, stack_of(half_a, act_ref, start, width))
        one = one + dot_nt(stack_of(half_d, d_ref, start, width), x_now)
        for t in range(start, start + width):
            ones = ones + tile(d_ref, t).astype(F32)
            twos = twos + g_tiles[t - start].astype(F32)
    held_one[...] = one
    held_two[...] = two
    line, _ = line_lanes(iota((C, 256), 1))
    d_l = d_lines[...]
    d_by_edge = jnp.concatenate([jnp.where(line == e, d_l, jnp.zeros_like(d_l)) for e in range(4)], axis=0)
    near_one[...] = dot_nt(d_by_edge, beside[...])
    near_two[...] = dot_nt(users[...], act_lines[...])

    def block_one(a, b):
        value = held_one[(2 - a) * C : (3 - a) * C, b * C : (b + 1) * C]
        for edge in range(4):
            for step in range(3):
                if tap_of(edge, step) == 3 * a + b:
                    value = value + near_one[edge * C : (edge + 1) * C, step * C : (step + 1) * C]
        return value

    def block_two(a, b):
        value = held_two[b * C : (b + 1) * C, a * C : (a + 1) * C]
        for edge in range(4):
            for step in range(3):
                if tap_of(edge, step) == 3 * a + b:
                    at = ((edge + 2) % 4) * 3 + step
                    value = value + near_two[at * C : (at + 1) * C, :]
        return value

    def whole(block, bias):
        tail = jnp.broadcast_to(jnp.sum(bias, axis=1, keepdims=True), (C, WIDE - BIAS_AT))
        return jnp.concatenate([block(a, b) for a in range(3) for b in range(3)] + [tail], axis=1)

    first = whole(block_one, ones)
    second = whole(block_two, twos)
    even = (lax.axis_index("space") % 2) == 0
    keep = jnp.where(even, first, second)
    give = jnp.where(even, second, first)
    share = C // parts
    for part in range(parts):
        at = slice(part * share, (part + 1) * share)
        mine[part] = jnp.concatenate([keep[at, j * LANES : (j + 1) * LANES] for j in range(WIDE // LANES)], axis=0)
        other[part] = jnp.concatenate([give[at, j * LANES : (j + 1) * LANES] for j in range(WIDE // LANES)], axis=0)


def inner_kernel(g_ref, d_ref, w_ref, d_in, half):
    zero = jnp.zeros((C, LANES), BF)
    half_shift(half, d_ref, zero, zero)

    def visit(t, value):
        at = slice(t * LANES, (t + 1) * LANES)
        d_in[:, at] = value + g_ref[:, at].astype(F32)

    conv_tiles(backward_form(float_taps(w_ref)), half, d_ref, None, visit)


def partial_kernel(x_ref, act_ref, w1_ref, w2_ref, bias, out, sides, back, half):
    taps = float_taps(w2_ref)
    wf = forward_form(taps)
    sides[0 : 2 * C] = row_form(taps)
    sides[2 * C :] = jnp.concatenate([wf[0:C], wf[2 * C : 3 * C]], axis=0)
    back[...] = return_form(float_taps(w1_ref))
    zero = jnp.zeros((C, LANES), BF)
    half_shift(half, act_ref, zero, zero)
    bias_now = bias[...]

    def visit(t, value):
        at = slice(t * LANES, (t + 1) * LANES)
        out[:, at] = value + bias_now + x_ref[:, at].astype(F32)

    conv_tiles(wf, half, act_ref, None, visit)


def finish_kernel(
    spaces, partial, d_in, m1, m2, n1, n2, halo, route, sides_ref, back,
    out_hbm, grad_in_hbm, out, grad_in, out_sem, grad_in_sem,
):
    lines, borders = by_edge(spaces, (m1, m2, n1, n2))
    rows, sides = edge_terms(sides_ref[2 * C :], sides_ref[0 : 2 * C], beside_lines(lines, halo))
    wide = PIX // CHUNKS
    copies = []

    def finish(src, dst, sem, before, row_terms, side_terms):
        for t in range(TILES):
            at = slice(t * LANES, (t + 1) * LANES)
            src[:, at] = add_edges(t, before[:, at], row_terms, side_terms).astype(BF)
            if (t + 1) % (TILES // CHUNKS) == 0:
                part = t // (TILES // CHUNKS)
                done = slice(part * wide, (part + 1) * wide)
                copies.append(pltpu.make_async_copy(src.at[:, done], dst.at[:, done], sem.at[part]))
                copies[-1].start()

    finish(out, out_hbm, out_sem, partial, rows, sides)
    line_grads = dot(back[...], users_values(route, borders))
    finish(grad_in, grad_in_hbm, grad_in_sem, d_in, line_grads[:, 0:LANES], line_grads[:, LANES:])
    for copy in copies:
        copy.wait()


def unpack_kernel(share, own, got, grad_one, bias_one, grad_two, bias_two):
    even = (lax.axis_index("space") % 2) == 0
    one = jnp.where(even, own[...], got[...])
    two = jnp.where(even, got[...], own[...])
    first, second = [
        jnp.concatenate([value[j * share : (j + 1) * share] for j in range(WIDE // LANES)], axis=1)
        for value in (one, two)
    ]
    eye = iota((share, LANES), 0) == iota((share, LANES), 1)
    for value, grad, bias in ((first, grad_one, bias_one), (second, grad_two, bias_two)):
        for tap in range(9):
            grad[tap] = value[:, tap * C : (tap + 1) * C]
        tail = jnp.broadcast_to(value[:, BIAS_AT : BIAS_AT + 1], (share, LANES))
        bias[...] = jnp.sum(jnp.where(eye, tail, 0.0), axis=0, keepdims=True)[:, 0:share]


def call(kernel, outs, specs, args, scratch=(), read=0, out_specs=None):
    return pl.pallas_call(
        kernel,
        out_shape=[jax.ShapeDtypeStruct(shape, dtype) for shape, dtype in outs],
        in_specs=specs,
        out_specs=out_specs or [VMEM] * len(outs),
        scratch_shapes=list(scratch),
        compiler_params=pltpu.CompilerParams(vmem_limit_bytes=16 * 2**20),
        cost_estimate=pl.CostEstimate(flops=0, bytes_accessed=read, transcendentals=0),
    )(*args)


HBM = pl.BlockSpec(memory_space=pltpu.HBM)


def in_hbm(value):
    return pltpu.with_memory_space_constraint(value, pltpu.HBM)


def swapped(block, mask, devices):
    return lax.ppermute(block, ("dp", "space"), [(i, i ^ mask) for i in range(devices)])


def swap_along(blocks, spaces, more=1):
    def second(i):
        return (i - 1) % spaces if i % 2 == 0 else (i + 1) % spaces

    return [
        lax.ppermute(blocks[0], "space", [(i, i ^ 1) for i in range(spaces)]),
        lax.ppermute(jnp.concatenate([blocks[1]] * more, axis=0) if more > 1 else blocks[1], "space", [(i, second(i)) for i in range(spaces)]),
    ]


def swap_across(blocks, spaces, devices):
    hop = spaces // 4
    return [swapped(blocks[0], hop, devices), swapped(blocks[1], hop ^ 2 * hop, devices)]


def first_rounds(parts, spaces):
    rounds = [[(True, 1 << bit)] for bit in reversed(range(parts.bit_length() - 1))]
    bit = 2
    while bit < spaces // 4:
        single = [r for r in rounds if len(r) == 1]
        if single:
            single[0].append((False, bit))
        else:
            rounds.append([(False, bit)])
        bit *= 2
    return rounds


def total_of(a, b, c, d):
    return (a.astype(F32) + b.astype(F32)) + (c.astype(F32) + d.astype(F32))


def last_round(held, blocks, spaces, devices, others):
    hop = spaces // 4
    held = held.astype(BF)
    joined = [jnp.concatenate([block, held], axis=0) for block in blocks]
    near, far = swap_across(joined, spaces, devices)
    opposite = swapped(held, 2 * hop, devices)
    held, *others = lax.optimization_barrier((held, *others))
    return near, far, total_of(held, near[C:], opposite, far[C:]), others


def reduced(held, bits, devices, spaces, beside):
    where = lax.axis_index("dp")
    keep = give = held.astype(BF)
    masks = []
    for is_part, bit in bits:
        masks.append(bit * spaces if is_part else bit)
        if is_part:
            upper = (where // bit) % 2 == 1
            low, high = keep[: keep.shape[0] // 2], keep[keep.shape[0] // 2 :]
            keep, give = jnp.where(upper, high, low), jnp.where(upper, low, high)
    first = swapped(give, masks[0], devices)
    kept, *beside = lax.optimization_barrier((keep, *beside))
    if len(masks) == 1:
        return kept.astype(F32) + first.astype(F32), beside
    return total_of(kept, first, swapped(keep, masks[1], devices), swapped(give, masks[0] ^ masks[1], devices)), beside


COST = 3_690_000


def on_device(inputs, cotangent, conv_one, bias_one, conv_two, bias_two, neighbours, corner_rule):
    parts = lax.axis_size("dp")
    spaces = lax.axis_size("space")
    share = C // parts
    x = inputs.reshape(C, PIX)
    g = cotangent.reshape(C, PIX)
    line = ((C, LANES), BF)
    image = ((C, PIX), BF)
    wide = ((C, PIX), F32)
    half = pltpu.VMEM((C, PIX + LANES), BF)
    tables = neighbours.transpose(2, 1, 0)
    rules = corner_rule.transpose(1, 0)

    weights = (conv_one.shape, BF)
    bias = ((C, LANES), F32)
    *sent, x_near, g_near = call(
        functools.partial(send_kernel, spaces), [line] * 4 + [image, image], [HBM] * 3, (in_hbm(tables), in_hbm(x), in_hbm(g)),
        [pltpu.SMEM(tables.shape, jnp.int32), pltpu.SemaphoreType.DMA, pltpu.SemaphoreType.DMA((CHUNKS,)),
         pltpu.SemaphoreType.DMA((CHUNKS,))],
        read=COST * 2,
    )
    devices = parts * spaces
    arrived = swap_along(sent[:2], spaces, 2) + swap_across(sent[2:], spaces, devices)
    edges = ((4 * C, 3 * C), BF)
    back = ((C, 12 * C), BF)
    d_act, pre_in, x_side, route, halo, w_edge, back2, w_one, w_two, b_one, b_two = call(
        functools.partial(prepare_kernel, spaces),
        [wide, wide, ((2 * C, PIX), BF), ((4, SIDE, 768), BF), ((256, 384), BF), edges, back,
         weights, weights, bias, bias],
        [HBM, HBM] + [VMEM] * 6,
        (in_hbm(tables), in_hbm(rules), x_near, g_near, conv_one, conv_two, bias_one.reshape(1, C), bias_two.reshape(1, C)),
        [half, pltpu.SMEM(tables.shape, jnp.int32), pltpu.SMEM(rules.shape, jnp.int32), pltpu.SemaphoreType.DMA((2,))],
        read=COST * 3,
    )
    middle = call(
        functools.partial(middle_kernel, spaces),
        [image, image] + [line] * 4 + [((3 * C, 256), BF), ((12 * C, 256), BF), ((C, 256), BF), ((C, 256), BF)],
        [HBM] + [VMEM] * 11,
        (in_hbm(tables), *arrived, d_act, pre_in, route, halo, w_edge, back2, b_one),
        [pltpu.SMEM(tables.shape, jnp.int32), pltpu.SemaphoreType.DMA],
        read=COST * 9 // 4,
    )
    act, d_pre = middle[:2]
    beside, users, act_lines, d_lines = middle[6:]
    packed = ((parts, share * WIDE // LANES, LANES), F32)
    mine, other = call(
        functools.partial(grads_kernel, parts), [packed, packed], [VMEM] * 9,
        (x, g, act, d_pre, x_side, beside, users, act_lines, d_lines),
        [half, half, pltpu.VMEM((3 * C, 3 * C), F32), pltpu.VMEM((3 * C, 3 * C), F32),
         pltpu.VMEM((4 * C, 3 * C), F32), pltpu.VMEM((12 * C, C), F32)],
        read=COST * 5 // 4,
    )
    (d_in,) = call(inner_kernel, [wide], [VMEM] * 3, (g, d_pre, w_one), [half], read=COST)
    partial, edges_two, back_one = call(
        partial_kernel, [wide, edges, back], [VMEM] * 5, (x, act, w_one, w_two, b_two), [half], read=COST * 3 // 2
    )
    held = mine + swapped(other, 1, devices)
    blocks = middle[2:6]
    again = swap_along(blocks[:2], spaces, 2)
    for bits in first_rounds(parts, spaces):
        held, again = reduced(held, bits, devices, spaces, again)
    near, far, own, (partial, d_in) = last_round(held[0], blocks[2:], spaces, devices, (partial, d_in))
    got = swapped(own, 1, devices)
    output, grad_in = call(
        functools.partial(finish_kernel, spaces), [image, image], [VMEM] * 10,
        (partial, d_in, *again, near, far, halo, route, edges_two, back_one),
        [pltpu.VMEM((C, PIX), BF), pltpu.VMEM((C, PIX), BF), pltpu.SemaphoreType.DMA((CHUNKS,)),
         pltpu.SemaphoreType.DMA((CHUNKS,))],
        read=COST * 3 // 2, out_specs=[HBM, HBM],
    )
    taps = ((9, share, C), F32)
    bias = ((1, share), F32)
    grad_one, sum_one, grad_two, sum_two = call(
        functools.partial(unpack_kernel, share), [taps, bias, taps, bias], [VMEM] * 2, (own, got), read=10**5
    )
    shape = inputs.shape
    return (
        output.reshape(shape),
        grad_in.reshape(shape),
        grad_one,
        sum_one.reshape(share),
        grad_two,
        sum_two.reshape(share),
    )


def solution(mesh):
    tiles = P("dp", "space", None, None)
    return jax.shard_map(
        on_device,
        mesh=mesh,
        in_specs=(tiles, tiles, P(), P(), P(), P(), P(), P()),
        out_specs=(tiles, tiles, P(None, "dp", None), P("dp"), P(None, "dp", None), P("dp")),
        check_vma=False,
    )
```

```python
import functools

import jax
import jax.numpy as jnp
from jax import lax
from jax.experimental import pallas as pl
from jax.experimental.pallas import tpu as pltpu
from jax.sharding import PartitionSpec as P

BF = jnp.bfloat16
F32 = jnp.float32
C = 48
SIDE = 64
PIX = SIDE * SIDE
LANES = 128
TILES = PIX // LANES

VMEM = pl.BlockSpec(memory_space=pltpu.VMEM)


def tap_of(edge, step):
    return (step, 3 * step + 2, 6 + step, 3 * step)[edge]


def offsets_of(spaces):
    return (-1, spaces // 4, 1, -(spaces // 4))


def dot(a, b):
    return jnp.dot(a, b, preferred_element_type=F32)


def dot_nt(a, b):
    return lax.dot_general(a, b, (((1,), (1,)), ((), ())), preferred_element_type=F32)


def iota(shape, axis):
    return lax.broadcasted_iota(jnp.int32, shape, axis)


def line_lanes(lane):
    z = lane - 128
    even = (z & 1) == 0
    left = jnp.where(z < 64, z, z - 63)
    right = jnp.where(z < 63, z + 2, jnp.where(z < 127, z - 63, 1))
    line = jnp.where(lane < 64, 0, jnp.where(lane < 128, 2, jnp.where(even, 3, 1)))
    place = jnp.where(lane < 64, lane, jnp.where(lane < 128, lane - 64, jnp.where(even, left, right)))
    return line, place


def lane_masks():
    lane = iota((C, LANES), 1) & 63
    return lane == 0, lane == 63


def tile(ref, t):
    return ref[:, t * LANES : (t + 1) * LANES]


def lines_from(tiles, first, last):
    total = tiles[0]
    for t in range(1, TILES):
        total = total + pltpu.roll(tiles[t], 2 * t, 1)
    low = iota((C, LANES), 1) < 64
    rows = jnp.where(low, first, last)
    return jnp.concatenate([rows, total], axis=1)


def edge_only(values):
    at_left, at_right = lane_masks()
    return jnp.where(at_left | at_right, values, jnp.zeros_like(values))


def roles(spaces):
    me = lax.axis_index("space")
    return me, (me % 2) == 0, ((me // (spaces // 4)) % 2) == 0


def swap_edges(even, inner):
    return (
        jnp.where(even, 0, 2),
        jnp.where(even, 2, 0),
        jnp.where(inner, 3, 1),
        jnp.where(inner, 1, 3),
    )


def send_choice(tables, spaces):
    me, even, inner = roles(spaces)
    hop = spaces // 4
    line, place = line_lanes(iota((256, 1), 0))
    lane = iota((1, LANES), 1)
    low = lane < 64
    spot = lane & 63
    chosen = []
    for edge in swap_edges(even, inner):
        offset = jnp.where(edge == 0, -1, jnp.where(edge == 1, hop, jnp.where(edge == 2, 1, -hop)))
        target = lax.rem(me - offset + spaces, spaces)
        k = tables[1, edge, target]
        r = tables[2, edge, target]
        turned = (r == 1) | (r == 2)
        wanted = jnp.where(low, k, lax.rem(edge + 2, 4)) * 64 + jnp.where(low & turned, 63 - spot, spot)
        chosen.append(jnp.where(line * 64 + place == wanted, 1.0, 0.0).astype(BF))
    return jnp.concatenate(chosen, axis=1)


def send_blocks(choice, field, border):
    moved = dot(jnp.concatenate([field, border], axis=0), choice)
    blocks = []
    for swap in range(4):
        at = slice(swap * LANES, (swap + 1) * LANES)
        blocks.append(jnp.where(iota((C, LANES), 1) < 64, moved[0:C, at], moved[C : 2 * C, at]).astype(BF))
    return blocks


def by_edge(spaces, swaps):
    _, even, inner = roles(spaces)
    m1, m2, n1, n2 = [ref[0:C] for ref in swaps]
    order = (
        jnp.where(even, m2, m1),
        jnp.where(inner, n1, n2),
        jnp.where(even, m1, m2),
        jnp.where(inner, n2, n1),
    )
    low = iota((C, LANES), 1) < 64
    turned = [pltpu.roll(block, 64, 1) for block in order]
    lines = [jnp.where(low, order[e], turned[e + 1]) for e in (0, 2)]
    return jnp.concatenate(lines, axis=1), [block[:, 0:64] for block in turned]


CHUNKS = 4


def send_kernel(
    spaces, tables_hbm, x_hbm, g_hbm, m1, m2, n1, n2, x_ref, g_ref, tables, table_sem, x_sem, g_sem,
):
    wide = PIX // CHUNKS
    fetch = pltpu.make_async_copy(tables_hbm, tables, table_sem)
    fetch.start()
    copies = []
    for part in range(CHUNKS):
        at = slice(part * wide, (part + 1) * wide)
        pair = [
            pltpu.make_async_copy(x_hbm.at[:, at], x_ref.at[:, at], x_sem.at[part]),
            pltpu.make_async_copy(g_hbm.at[:, at], g_ref.at[:, at], g_sem.at[part]),
        ]
        for copy in pair:
            copy.start()
        copies.append(pair)
    fetch.wait()
    choice = send_choice(tables, spaces)
    parts = [[], []]
    for part in range(CHUNKS):
        for field, ref in enumerate((x_ref, g_ref)):
            copies[part][field].wait()
            for t in range(part * TILES // CHUNKS, (part + 1) * TILES // CHUNKS):
                parts[field].append(edge_only(tile(ref, t)))
    both = [
        lines_from(parts[field], tile(ref, 0), tile(ref, TILES - 1))
        for field, ref in enumerate((x_ref, g_ref))
    ]
    for out, block in zip((m1, m2, n1, n2), send_blocks(choice, *both)):
        out[...] = block


def weights_of(rules, where, corner):
    rule = rules[corner, where]
    first = jnp.where(rule == 0, 1.0, jnp.where(rule == 1, 0.0, 0.5)).astype(F32)
    return first, 1.0 - first


def user_matrix(tables, rules, me, spaces, edge, step):
    used = (edge + 2) % 4
    user = lax.rem(me + offsets_of(spaces)[edge] + spaces, spaces)
    k = tables[1, used, user]
    r = tables[2, used, user]
    turned = (r == 1) | (r == 2)
    q = iota((SIDE, 256), 0)
    line, place = line_lanes(iota((1, 256), 1))
    want = jnp.where(turned, 63 - place, place)
    mine = line == k
    value = jnp.where(mine & (q == want + 1 - step), 1.0, 0.0)
    which = used % 2
    corners = ((0, 1), (1, 3), (2, 3), (0, 2))[used]
    if step == 0:
        weight = weights_of(rules, user, corners[0])[which]
        value = value + jnp.where(mine & (want == 0) & (q == 0), weight, 0.0)
    if step == 2:
        weight = weights_of(rules, user, corners[1])[which]
        value = value + jnp.where(mine & (want == 63) & (q == 63), weight, 0.0)
    return value.astype(BF)


def halo_matrix(rules, me, step):
    row = iota((256, LANES), 0)
    line, place = line_lanes(iota((1, LANES), 1) + LANES)
    at = place + step - 1
    inside = (at >= 0) & (at < 64)
    value = jnp.where(inside & (row == line * 64 + at), 1.0, 0.0)
    left = line == 3
    if step != 1:
        if step == 0:
            active = place == 0
            row_a = jnp.where(left, 0, 63)
            row_b = jnp.where(left, 192, 64)
            pair = (0, 1)
        else:
            active = place == 63
            row_a = jnp.where(left, 128, 191)
            row_b = jnp.where(left, 255, 127)
            pair = (2, 3)
        fl, sl = weights_of(rules, me, pair[0])
        fr, sr = weights_of(rules, me, pair[1])
        value = value + jnp.where(active & (row == row_a), jnp.where(left, fl, fr), 0.0)
        value = value + jnp.where(active & (row == row_b), jnp.where(left, sl, sr), 0.0)
    return value.astype(BF)


def beside_lines(lines, halo):
    columns = dot(lines, halo[...]).astype(BF)
    low = iota((C, LANES), 1) < 64
    at_left, at_right = lane_masks()
    rows = jnp.where(low, lines[:, 0:LANES], pltpu.roll(lines[:, LANES:], 64, 1))
    none = jnp.zeros_like(rows)
    moved = (
        jnp.where(at_left, none, pltpu.roll(rows, 1, 1)),
        rows,
        jnp.where(at_right, none, pltpu.roll(rows, LANES - 1, 1)),
    )
    parts = [
        jnp.concatenate([moved[s], columns[:, s * LANES : (s + 1) * LANES]], axis=1) for s in range(3)
    ]
    return jnp.concatenate(parts, axis=0)


def half_shift(dst, ref, before, after):
    low = iota((C, LANES), 1) < 64
    for t in range(TILES + 1):
        here = tile(ref, t) if t < TILES else after
        prev = tile(ref, t - 1) if t > 0 else before
        mixed = jnp.where(low, here.astype(F32), prev.astype(F32))
        dst[:, t * LANES : (t + 1) * LANES] = pltpu.roll(mixed, 64, 1).astype(BF)


def stack_of(half, ref, start, width):
    at = start * LANES
    size = width * LANES
    return jnp.concatenate(
        [half[:, at : at + size], ref[:, at : at + size], half[:, at + LANES : at + LANES + size]], axis=0
    )


def conv_tiles(weights, half, ref, columns, visit):
    at_left, at_right = lane_masks()
    for chunk in range(TILES // 2):
        taps = dot(weights, stack_of(half, ref, 2 * chunk, 2))
        for part in range(2):
            t = 2 * chunk + part
            lanes = slice(part * LANES, (part + 1) * LANES)
            side = 0.0 if columns is None else pltpu.roll(columns, (LANES - 2 * t) % LANES, 1)
            left = jnp.where(at_left, side, pltpu.roll(taps[0:C, lanes], 1, 1))
            right = jnp.where(at_right, side, pltpu.roll(taps[2 * C : 3 * C, lanes], LANES - 1, 1))
            visit(t, taps[C : 2 * C, lanes] + left + right)


def block_rows(taps, order):
    return jnp.concatenate([jnp.concatenate([taps[t] for t in row], axis=1) for row in order], axis=0)


def forward_form(taps):
    return block_rows(taps, [[b, 3 + b, 6 + b] for b in range(3)]).astype(BF)


def backward_form(taps):
    return block_rows(taps, [[8 - 3 * a - b for b in range(3)] for a in range(3)]).T.astype(BF)


def row_form(taps):
    return block_rows(taps, [[0, 1, 2], [6, 7, 8]]).astype(BF)


def return_form(taps):
    order = [[tap_of((edge + 2) % 4, step)] for edge in range(4) for step in range(3)]
    return block_rows(taps, order).T.astype(BF)


def float_taps(ref):
    return [ref[t].astype(F32) for t in range(9)]


def column(bias):
    row = jnp.broadcast_to(bias[...], (C, C))
    eye = iota((C, C), 0) == iota((C, C), 1)
    return jnp.broadcast_to(jnp.sum(jnp.where(eye, row, 0.0), axis=1, keepdims=True), (C, LANES))


def prepare_kernel(
    spaces, tables_hbm, rules_hbm, x_ref, g_ref, w1_ref, w2_ref, b1_ref, b2_ref,
    d_act, pre_in, x_side, route, halo, w_edge, back2, w1_out, w2_out, b1_out, b2_out,
    half, tables, rules, table_sem,
):
    fetches = [
        pltpu.make_async_copy(tables_hbm, tables, table_sem.at[0]),
        pltpu.make_async_copy(rules_hbm, rules, table_sem.at[1]),
    ]
    for fetch in fetches:
        fetch.start()
    me = lax.axis_index("space")
    taps1 = float_taps(w1_ref)
    taps2 = float_taps(w2_ref)
    wf1 = forward_form(taps1)
    w_edge[0 : 2 * C] = row_form(taps1)
    w_edge[2 * C :] = jnp.concatenate([wf1[0:C], wf1[2 * C : 3 * C]], axis=0)
    back2[...] = return_form(taps2)
    w1_out[...] = w1_ref[...]
    w2_out[...] = w2_ref[...]
    b1_out[...] = column(b1_ref)
    b2_out[...] = column(b2_ref)
    zero = jnp.zeros((C, LANES), BF)
    half_shift(half, g_ref, zero, zero)

    def keep(ref):
        def visit(t, value):
            ref[:, t * LANES : (t + 1) * LANES] = value

        return visit

    conv_tiles(backward_form(taps2), half, g_ref, None, keep(d_act))
    half_shift(half, x_ref, zero, zero)
    conv_tiles(wf1, half, x_ref, None, keep(pre_in))
    at_left, at_right = lane_masks()
    for t in range(TILES):
        at = slice(t * LANES, (t + 1) * LANES)
        x = tile(x_ref, t).astype(F32)
        x_side[0:C, at] = jnp.where(at_left, 0.0, pltpu.roll(x, 1, 1)).astype(BF)
        x_side[C : 2 * C, at] = jnp.where(at_right, 0.0, pltpu.roll(x, LANES - 1, 1)).astype(BF)
    for fetch in fetches:
        fetch.wait()
    for edge in range(4):
        for step in range(3):
            route[edge, :, step * 256 : (step + 1) * 256] = user_matrix(tables, rules, me, spaces, edge, step)
    for step in range(3):
        halo[:, step * LANES : (step + 1) * LANES] = halo_matrix(rules, me, step)


def edge_terms(w_sides, w_rows, stacked):
    rows = dot(w_rows, stacked[:, 0:LANES])
    sides = dot(w_sides, stacked[:, LANES:])
    lane = iota((C, LANES), 1)
    rows = jnp.where(lane < 64, rows[0:C], rows[C : 2 * C])
    return rows, jnp.where((lane & 1) == 0, sides[0:C], sides[C : 2 * C])


def add_edges(t, value, rows, sides):
    at_left, at_right = lane_masks()
    low = iota((C, LANES), 1) < 64
    value = value + jnp.where(at_left | at_right, pltpu.roll(sides, (LANES - 2 * t) % LANES, 1), 0.0)
    if t == 0:
        value = value + jnp.where(low, rows, 0.0)
    if t == TILES - 1:
        value = value + jnp.where(low, 0.0, rows)
    return value


def users_values(route, borders):
    parts = []
    for edge in range(4):
        moved = dot(borders[edge], route[edge]).astype(BF)
        parts += [moved[:, s * 256 : (s + 1) * 256] for s in range(3)]
    return jnp.concatenate(parts, axis=0)


def middle_kernel(
    spaces, tables_hbm, m1, m2, n1, n2, d_act, pre_in, route, halo, w_edge, back, bias,
    act_ref, d_ref, p0, p1, p2, p3, beside_ref, users_ref, act_lines, d_lines, tables, table_sem,
):
    fetch = pltpu.make_async_copy(tables_hbm, tables, table_sem)
    fetch.start()
    lines, borders = by_edge(spaces, (m1, m2, n1, n2))
    beside = beside_lines(lines, halo)
    beside_ref[...] = beside
    rows, sides = edge_terms(w_edge[2 * C :], w_edge[0 : 2 * C], beside)
    users = users_values(route, borders)
    users_ref[...] = users
    line_grads = dot(back[...], users)
    d_rows = line_grads[:, 0:LANES]
    d_sides = line_grads[:, LANES : 2 * LANES]
    bias_now = bias[...]
    act_edges = []
    d_edges = []
    ends = {}
    for t in range(TILES):
        at = slice(t * LANES, (t + 1) * LANES)
        pre = add_edges(t, pre_in[:, at], rows, sides) + bias_now
        square = pre * pre
        inner = 0.7978845608028654 * pre * (1.0 + 0.044715 * square)
        wave = jnp.tanh(inner)
        cdf = 0.5 + 0.5 * wave
        slope = cdf + 0.5 * pre * (1.0 - wave * wave) * (0.7978845608028654 + 0.1070322243 * square)
        grad = add_edges(t, d_act[:, at], d_rows, d_sides)
        act = (pre * cdf).astype(BF)
        d_pre = (grad * slope).astype(BF)
        act_ref[:, at] = act
        d_ref[:, at] = d_pre
        act_edges.append(edge_only(act))
        d_edges.append(edge_only(d_pre))
        if t in (0, TILES - 1):
            ends[t] = (act, d_pre)
    act_l = lines_from(act_edges, ends[0][0], ends[TILES - 1][0])
    d_l = lines_from(d_edges, ends[0][1], ends[TILES - 1][1])
    act_lines[...] = act_l
    d_lines[...] = d_l
    fetch.wait()
    for out, block in zip((p0, p1, p2, p3), send_blocks(send_choice(tables, spaces), act_l, d_l)):
        out[...] = block


WIDE = 512
BIAS_AT = 9 * C


def grads_kernel(
    parts, x_ref, g_ref, act_ref, d_ref, x_side, beside, users, act_lines, d_lines,
    mine, other, half_a, half_d, held_one, held_two, near_one, near_two,
):
    zero = jnp.zeros((C, LANES), BF)
    half_shift(half_a, act_ref, zero, zero)
    half_shift(half_d, d_ref, zero, zero)
    width = 4
    at_left, at_right = lane_masks()
    one = jnp.zeros((3 * C, 3 * C), F32)
    two = jnp.zeros((3 * C, 3 * C), F32)
    ones = jnp.zeros((C, LANES), F32)
    twos = jnp.zeros((C, LANES), F32)
    for start in range(0, TILES, width):
        at = slice(start * LANES, (start + width) * LANES)
        g_tiles = [tile(g_ref, t) for t in range(start, start + width)]
        after = [jnp.where(at_right, zero, pltpu.roll(g, LANES - 1, 1)) for g in g_tiles]
        before = [jnp.where(at_left, zero, pltpu.roll(g, 1, 1)) for g in g_tiles]
        g_now = [jnp.concatenate(after, axis=1), g_ref[:, at], jnp.concatenate(before, axis=1)]
        g_now = jnp.concatenate(g_now, axis=0)
        x_now = jnp.concatenate([x_side[0:C, at], x_ref[:, at], x_side[C : 2 * C, at]], axis=0)
        two = two + dot_nt(g_now, stack_of(half_a, act_ref, start, width))
        one = one + dot_nt(stack_of(half_d, d_ref, start, width), x_now)
        for t in range(start, start + width):
            ones = ones + tile(d_ref, t).astype(F32)
            twos = twos + g_tiles[t - start].astype(F32)
    held_one[...] = one
    held_two[...] = two
    line, _ = line_lanes(iota((C, 256), 1))
    d_l = d_lines[...]
    d_by_edge = jnp.concatenate([jnp.where(line == e, d_l, jnp.zeros_like(d_l)) for e in range(4)], axis=0)
    near_one[...] = dot_nt(d_by_edge, beside[...])
    near_two[...] = dot_nt(users[...], act_lines[...])

    def block_one(a, b):
        value = held_one[(2 - a) * C : (3 - a) * C, b * C : (b + 1) * C]
        for edge in range(4):
            for step in range(3):
                if tap_of(edge, step) == 3 * a + b:
                    value = value + near_one[edge * C : (edge + 1) * C, step * C : (step + 1) * C]
        return value

    def block_two(a, b):
        value = held_two[b * C : (b + 1) * C, a * C : (a + 1) * C]
        for edge in range(4):
            for step in range(3):
                if tap_of(edge, step) == 3 * a + b:
                    at = ((edge + 2) % 4) * 3 + step
                    value = value + near_two[at * C : (at + 1) * C, :]
        return value

    def whole(block, bias):
        tail = jnp.broadcast_to(jnp.sum(bias, axis=1, keepdims=True), (C, WIDE - BIAS_AT))
        return jnp.concatenate([block(a, b) for a in range(3) for b in range(3)] + [tail], axis=1)

    first = whole(block_one, ones)
    second = whole(block_two, twos)
    even = (lax.axis_index("space") % 2) == 0
    keep = jnp.where(even, first, second)
    give = jnp.where(even, second, first)
    share = C // parts
    for part in range(parts):
        at = slice(part * share, (part + 1) * share)
        mine[part] = jnp.concatenate([keep[at, j * LANES : (j + 1) * LANES] for j in range(WIDE // LANES)], axis=0)
        other[part] = jnp.concatenate([give[at, j * LANES : (j + 1) * LANES] for j in range(WIDE // LANES)], axis=0)


def inner_kernel(g_ref, d_ref, w_ref, d_in, half):
    zero = jnp.zeros((C, LANES), BF)
    half_shift(half, d_ref, zero, zero)

    def visit(t, value):
        at = slice(t * LANES, (t + 1) * LANES)
        d_in[:, at] = value + g_ref[:, at].astype(F32)

    conv_tiles(backward_form(float_taps(w_ref)), half, d_ref, None, visit)


def partial_kernel(x_ref, act_ref, w1_ref, w2_ref, bias, out, sides, back, half):
    taps = float_taps(w2_ref)
    wf = forward_form(taps)
    sides[0 : 2 * C] = row_form(taps)
    sides[2 * C :] = jnp.concatenate([wf[0:C], wf[2 * C : 3 * C]], axis=0)
    back[...] = return_form(float_taps(w1_ref))
    zero = jnp.zeros((C, LANES), BF)
    half_shift(half, act_ref, zero, zero)
    bias_now = bias[...]

    def visit(t, value):
        at = slice(t * LANES, (t + 1) * LANES)
        out[:, at] = value + bias_now + x_ref[:, at].astype(F32)

    conv_tiles(wf, half, act_ref, None, visit)


def finish_kernel(
    spaces, partial, d_in, m1, m2, n1, n2, halo, route, sides_ref, back,
    out_hbm, grad_in_hbm, out, grad_in, out_sem, grad_in_sem,
):
    lines, borders = by_edge(spaces, (m1, m2, n1, n2))
    rows, sides = edge_terms(sides_ref[2 * C :], sides_ref[0 : 2 * C], beside_lines(lines, halo))
    wide = PIX // CHUNKS
    copies = []

    def finish(src, dst, sem, before, row_terms, side_terms):
        for t in range(TILES):
            at = slice(t * LANES, (t + 1) * LANES)
            src[:, at] = add_edges(t, before[:, at], row_terms, side_terms).astype(BF)
            if (t + 1) % (TILES // CHUNKS) == 0:
                part = t // (TILES // CHUNKS)
                done = slice(part * wide, (part + 1) * wide)
                copies.append(pltpu.make_async_copy(src.at[:, done], dst.at[:, done], sem.at[part]))
                copies[-1].start()

    finish(out, out_hbm, out_sem, partial, rows, sides)
    line_grads = dot(back[...], users_values(route, borders))
    finish(grad_in, grad_in_hbm, grad_in_sem, d_in, line_grads[:, 0:LANES], line_grads[:, LANES:])
    for copy in copies:
        copy.wait()


def unpack_kernel(share, own, got, grad_one, bias_one, grad_two, bias_two):
    even = (lax.axis_index("space") % 2) == 0
    one = jnp.where(even, own[...], got[...])
    two = jnp.where(even, got[...], own[...])
    first, second = [
        jnp.concatenate([value[j * share : (j + 1) * share] for j in range(WIDE // LANES)], axis=1)
        for value in (one, two)
    ]
    eye = iota((share, LANES), 0) == iota((share, LANES), 1)
    for value, grad, bias in ((first, grad_one, bias_one), (second, grad_two, bias_two)):
        for tap in range(9):
            grad[tap] = value[:, tap * C : (tap + 1) * C]
        tail = jnp.broadcast_to(value[:, BIAS_AT : BIAS_AT + 1], (share, LANES))
        bias[...] = jnp.sum(jnp.where(eye, tail, 0.0), axis=0, keepdims=True)[:, 0:share]


def call(kernel, outs, specs, args, scratch=(), read=0, out_specs=None):
    return pl.pallas_call(
        kernel,
        out_shape=[jax.ShapeDtypeStruct(shape, dtype) for shape, dtype in outs],
        in_specs=specs,
        out_specs=out_specs or [VMEM] * len(outs),
        scratch_shapes=list(scratch),
        compiler_params=pltpu.CompilerParams(vmem_limit_bytes=16 * 2**20),
        cost_estimate=pl.CostEstimate(flops=0, bytes_accessed=read, transcendentals=0),
    )(*args)


HBM = pl.BlockSpec(memory_space=pltpu.HBM)


def in_hbm(value):
    return pltpu.with_memory_space_constraint(value, pltpu.HBM)


def swapped(block, mask, devices):
    return lax.ppermute(block, ("dp", "space"), [(i, i ^ mask) for i in range(devices)])


def swap_along(blocks, spaces, more=1):
    def second(i):
        return (i - 1) % spaces if i % 2 == 0 else (i + 1) % spaces

    return [
        lax.ppermute(blocks[0], "space", [(i, i ^ 1) for i in range(spaces)]),
        lax.ppermute(jnp.concatenate([blocks[1]] * more, axis=0) if more > 1 else blocks[1], "space", [(i, second(i)) for i in range(spaces)]),
    ]


def swap_across(blocks, spaces, devices):
    hop = spaces // 4
    return [swapped(blocks[0], hop, devices), swapped(blocks[1], hop ^ 2 * hop, devices)]


def first_rounds(parts, spaces):
    rounds = [[(True, 1 << bit)] for bit in reversed(range(parts.bit_length() - 1))]
    bit = 2
    while bit < spaces // 4:
        single = [r for r in rounds if len(r) == 1]
        if single:
            single[0].append((False, bit))
        else:
            rounds.append([(False, bit)])
        bit *= 2
    return rounds


def total_of(a, b, c, d):
    return (a.astype(F32) + b.astype(F32)) + (c.astype(F32) + d.astype(F32))


def last_round(held, blocks, spaces, devices, others):
    hop = spaces // 4
    held = held.astype(BF)
    joined = [jnp.concatenate([block, held], axis=0) for block in blocks]
    near, far = swap_across(joined, spaces, devices)
    opposite = swapped(held, 2 * hop, devices)
    held, *others = lax.optimization_barrier((held, *others))
    return near, far, total_of(held, near[C:], opposite, far[C:]), others


def reduced(held, bits, devices, spaces):
    where = lax.axis_index("dp")
    keep = give = held.astype(BF)
    masks = []
    for is_part, bit in bits:
        masks.append(bit * spaces if is_part else bit)
        if is_part:
            upper = (where // bit) % 2 == 1
            low, high = keep[: keep.shape[0] // 2], keep[keep.shape[0] // 2 :]
            keep, give = jnp.where(upper, high, low), jnp.where(upper, low, high)
    first = swapped(give, masks[0], devices)
    if len(masks) == 1:
        return keep.astype(F32) + first.astype(F32)
    return total_of(keep, first, swapped(keep, masks[1], devices), swapped(give, masks[0] ^ masks[1], devices))


COST = 3_690_000


def on_device(inputs, cotangent, conv_one, bias_one, conv_two, bias_two, neighbours, corner_rule):
    parts = lax.axis_size("dp")
    spaces = lax.axis_size("space")
    share = C // parts
    x = inputs.reshape(C, PIX)
    g = cotangent.reshape(C, PIX)
    line = ((C, LANES), BF)
    image = ((C, PIX), BF)
    wide = ((C, PIX), F32)
    half = pltpu.VMEM((C, PIX + LANES), BF)
    tables = neighbours.transpose(2, 1, 0)
    rules = corner_rule.transpose(1, 0)

    weights = (conv_one.shape, BF)
    bias = ((C, LANES), F32)
    *sent, x_near, g_near = call(
        functools.partial(send_kernel, spaces), [line] * 4 + [image, image], [HBM] * 3, (in_hbm(tables), in_hbm(x), in_hbm(g)),
        [pltpu.SMEM(tables.shape, jnp.int32), pltpu.SemaphoreType.DMA, pltpu.SemaphoreType.DMA((CHUNKS,)),
         pltpu.SemaphoreType.DMA((CHUNKS,))],
        read=COST * 2,
    )
    devices = parts * spaces
    arrived = swap_along(sent[:2], spaces, 2) + swap_across(sent[2:], spaces, devices)
    edges = ((4 * C, 3 * C), BF)
    back = ((C, 12 * C), BF)
    d_act, pre_in, x_side, route, halo, w_edge, back2, w_one, w_two, b_one, b_two = call(
        functools.partial(prepare_kernel, spaces),
        [wide, wide, ((2 * C, PIX), BF), ((4, SIDE, 768), BF), ((256, 384), BF), edges, back,
         weights, weights, bias, bias],
        [HBM, HBM] + [VMEM] * 6,
        (in_hbm(tables), in_hbm(rules), x_near, g_near, conv_one, conv_two, bias_one.reshape(1, C), bias_two.reshape(1, C)),
        [half, pltpu.SMEM(tables.shape, jnp.int32), pltpu.SMEM(rules.shape, jnp.int32), pltpu.SemaphoreType.DMA((2,))],
        read=COST * 3,
    )
    middle = call(
        functools.partial(middle_kernel, spaces),
        [image, image] + [line] * 4 + [((3 * C, 256), BF), ((12 * C, 256), BF), ((C, 256), BF), ((C, 256), BF)],
        [HBM] + [VMEM] * 11,
        (in_hbm(tables), *arrived, d_act, pre_in, route, halo, w_edge, back2, b_one),
        [pltpu.SMEM(tables.shape, jnp.int32), pltpu.SemaphoreType.DMA],
        read=COST * 9 // 4,
    )
    act, d_pre = middle[:2]
    beside, users, act_lines, d_lines = middle[6:]
    packed = ((parts, share * WIDE // LANES, LANES), F32)
    mine, other = call(
        functools.partial(grads_kernel, parts), [packed, packed], [VMEM] * 9,
        (x, g, act, d_pre, x_side, beside, users, act_lines, d_lines),
        [half, half, pltpu.VMEM((3 * C, 3 * C), F32), pltpu.VMEM((3 * C, 3 * C), F32),
         pltpu.VMEM((4 * C, 3 * C), F32), pltpu.VMEM((12 * C, C), F32)],
        read=COST * 5 // 4,
    )
    blocks = middle[2:6]
    again = swap_along(blocks[:2], spaces, 3)
    act_late, d_late, *again = lax.optimization_barrier((act, d_pre, *again))
    (d_in,) = call(inner_kernel, [wide], [VMEM] * 3, (g, d_late, w_one), [half], read=COST)
    partial, edges_two, back_one = call(
        partial_kernel, [wide, edges, back], [VMEM] * 5, (x, act_late, w_one, w_two, b_two), [half], read=COST * 3 // 2
    )
    held = mine + swapped(other, 1, devices)
    for bits in first_rounds(parts, spaces):
        held = reduced(held, bits, devices, spaces)
    near, far, own, (partial, d_in) = last_round(held[0], blocks[2:], spaces, devices, (partial, d_in))
    got = swapped(own, 1, devices)
    output, grad_in = call(
        functools.partial(finish_kernel, spaces), [image, image], [VMEM] * 10,
        (partial, d_in, *again, near, far, halo, route, edges_two, back_one),
        [pltpu.VMEM((C, PIX), BF), pltpu.VMEM((C, PIX), BF), pltpu.SemaphoreType.DMA((CHUNKS,)),
         pltpu.SemaphoreType.DMA((CHUNKS,))],
        read=COST * 3 // 2, out_specs=[HBM, HBM],
    )
    taps = ((9, share, C), F32)
    bias = ((1, share), F32)
    grad_one, sum_one, grad_two, sum_two = call(
        functools.partial(unpack_kernel, share), [taps, bias, taps, bias], [VMEM] * 2, (own, got), read=10**5
    )
    shape = inputs.shape
    return (
        output.reshape(shape),
        grad_in.reshape(shape),
        grad_one,
        sum_one.reshape(share),
        grad_two,
        sum_two.reshape(share),
    )


def solution(mesh):
    tiles = P("dp", "space", None, None)
    return jax.shard_map(
        on_device,
        mesh=mesh,
        in_specs=(tiles, tiles, P(), P(), P(), P(), P(), P()),
        out_specs=(tiles, tiles, P(None, "dp", None), P("dp"), P(None, "dp", None), P("dp")),
        check_vma=False,
    )
```

```python
import functools

import jax
import jax.numpy as jnp
from jax import lax
from jax.experimental import pallas as pl
from jax.experimental.pallas import tpu as pltpu
from jax.sharding import PartitionSpec as P

BF = jnp.bfloat16
F32 = jnp.float32
C = 48
SIDE = 64
PIX = SIDE * SIDE
LANES = 128
TILES = PIX // LANES

VMEM = pl.BlockSpec(memory_space=pltpu.VMEM)


def tap_of(edge, step):
    return (step, 3 * step + 2, 6 + step, 3 * step)[edge]


def offsets_of(spaces):
    return (-1, spaces // 4, 1, -(spaces // 4))


def dot(a, b):
    return jnp.dot(a, b, preferred_element_type=F32)


def dot_nt(a, b):
    return lax.dot_general(a, b, (((1,), (1,)), ((), ())), preferred_element_type=F32)


def iota(shape, axis):
    return lax.broadcasted_iota(jnp.int32, shape, axis)


def line_lanes(lane):
    z = lane - 128
    even = (z & 1) == 0
    left = jnp.where(z < 64, z, z - 63)
    right = jnp.where(z < 63, z + 2, jnp.where(z < 127, z - 63, 1))
    line = jnp.where(lane < 64, 0, jnp.where(lane < 128, 2, jnp.where(even, 3, 1)))
    place = jnp.where(lane < 64, lane, jnp.where(lane < 128, lane - 64, jnp.where(even, left, right)))
    return line, place


def lane_masks():
    lane = iota((C, LANES), 1) & 63
    return lane == 0, lane == 63


def tile(ref, t):
    return ref[:, t * LANES : (t + 1) * LANES]


def lines_from(tiles, first, last):
    total = tiles[0]
    for t in range(1, TILES):
        total = total + pltpu.roll(tiles[t], 2 * t, 1)
    low = iota((C, LANES), 1) < 64
    rows = jnp.where(low, first, last)
    return jnp.concatenate([rows, total], axis=1)


def edge_only(values):
    at_left, at_right = lane_masks()
    return jnp.where(at_left | at_right, values, jnp.zeros_like(values))


def roles(spaces):
    me = lax.axis_index("space")
    return me, (me % 2) == 0, ((me // (spaces // 4)) % 2) == 0


def swap_edges(even, inner):
    return (
        jnp.where(even, 0, 2),
        jnp.where(even, 2, 0),
        jnp.where(inner, 3, 1),
        jnp.where(inner, 1, 3),
    )


def send_choice(tables, spaces):
    me, even, inner = roles(spaces)
    hop = spaces // 4
    line, place = line_lanes(iota((256, LANES), 0))
    code = line * 64 + place
    lane = iota((1, LANES), 1)
    low = lane < 64
    spot = lane & 63
    chosen = []
    for edge in swap_edges(even, inner):
        offset = jnp.where(edge == 0, -1, jnp.where(edge == 1, hop, jnp.where(edge == 2, 1, -hop)))
        target = lax.rem(me - offset + spaces, spaces)
        k = tables[1, edge, target]
        r = tables[2, edge, target]
        turned = (r == 1) | (r == 2)
        wanted = jnp.where(low, k, lax.rem(edge + 2, 4)) * 64 + jnp.where(low & turned, 63 - spot, spot)
        chosen.append(jnp.where(code == wanted, 1.0, 0.0).astype(BF))
    return jnp.concatenate(chosen, axis=1)


def send_blocks(choice, field, border):
    moved = dot(jnp.concatenate([field, border], axis=0), choice)
    blocks = []
    for swap in range(4):
        at = slice(swap * LANES, (swap + 1) * LANES)
        blocks.append(jnp.where(iota((C, LANES), 1) < 64, moved[0:C, at], moved[C : 2 * C, at]).astype(BF))
    return blocks


def by_edge(spaces, swaps):
    _, even, inner = roles(spaces)
    m1, m2, n1, n2 = [ref[0:C] for ref in swaps]
    order = (
        jnp.where(even, m2, m1),
        jnp.where(inner, n1, n2),
        jnp.where(even, m1, m2),
        jnp.where(inner, n2, n1),
    )
    low = iota((C, LANES), 1) < 64
    turned = [pltpu.roll(block, 64, 1) for block in order]
    lines = [jnp.where(low, order[e], turned[e + 1]) for e in (0, 2)]
    return jnp.concatenate(lines, axis=1), [block[:, 0:64] for block in turned]


CHUNKS = 4


def send_kernel(
    spaces, tables_hbm, x_hbm, g_hbm, m1, m2, n1, n2, x_ref, g_ref, choice_out, tables, table_sem, x_sem, g_sem,
):
    wide = PIX // CHUNKS
    fetch = pltpu.make_async_copy(tables_hbm, tables, table_sem)
    fetch.start()
    copies = []
    for part in range(CHUNKS):
        at = slice(part * wide, (part + 1) * wide)
        pair = [
            pltpu.make_async_copy(x_hbm.at[:, at], x_ref.at[:, at], x_sem.at[part]),
            pltpu.make_async_copy(g_hbm.at[:, at], g_ref.at[:, at], g_sem.at[part]),
        ]
        for copy in pair:
            copy.start()
        copies.append(pair)
    fetch.wait()
    choice = send_choice(tables, spaces)
    choice_out[...] = choice
    parts = [[], []]
    for part in range(CHUNKS):
        for field, ref in enumerate((x_ref, g_ref)):
            copies[part][field].wait()
            for t in range(part * TILES // CHUNKS, (part + 1) * TILES // CHUNKS):
                parts[field].append(edge_only(tile(ref, t)))
    both = [
        lines_from(parts[field], tile(ref, 0), tile(ref, TILES - 1))
        for field, ref in enumerate((x_ref, g_ref))
    ]
    for out, block in zip((m1, m2, n1, n2), send_blocks(choice, *both)):
        out[...] = block


def weights_of(rules, where, corner):
    rule = rules[corner, where]
    first = jnp.where(rule == 0, 1.0, jnp.where(rule == 1, 0.0, 0.5)).astype(F32)
    return first, 1.0 - first


def user_matrix(tables, rules, me, spaces, edge, step):
    used = (edge + 2) % 4
    user = lax.rem(me + offsets_of(spaces)[edge] + spaces, spaces)
    k = tables[1, used, user]
    r = tables[2, used, user]
    turned = (r == 1) | (r == 2)
    q = iota((SIDE, 256), 0)
    line, place = line_lanes(iota((1, 256), 1))
    want = jnp.where(turned, 63 - place, place)
    mine = line == k
    value = jnp.where(mine & (q == want + 1 - step), 1.0, 0.0)
    which = used % 2
    corners = ((0, 1), (1, 3), (2, 3), (0, 2))[used]
    if step == 0:
        weight = weights_of(rules, user, corners[0])[which]
        value = value + jnp.where(mine & (want == 0) & (q == 0), weight, 0.0)
    if step == 2:
        weight = weights_of(rules, user, corners[1])[which]
        value = value + jnp.where(mine & (want == 63) & (q == 63), weight, 0.0)
    return value.astype(BF)


def halo_matrix(rules, me, step):
    row = iota((256, LANES), 0)
    line, place = line_lanes(iota((1, LANES), 1) + LANES)
    at = place + step - 1
    inside = (at >= 0) & (at < 64)
    value = jnp.where(inside & (row == line * 64 + at), 1.0, 0.0)
    left = line == 3
    if step != 1:
        if step == 0:
            active = place == 0
            row_a = jnp.where(left, 0, 63)
            row_b = jnp.where(left, 192, 64)
            pair = (0, 1)
        else:
            active = place == 63
            row_a = jnp.where(left, 128, 191)
            row_b = jnp.where(left, 255, 127)
            pair = (2, 3)
        fl, sl = weights_of(rules, me, pair[0])
        fr, sr = weights_of(rules, me, pair[1])
        value = value + jnp.where(active & (row == row_a), jnp.where(left, fl, fr), 0.0)
        value = value + jnp.where(active & (row == row_b), jnp.where(left, sl, sr), 0.0)
    return value.astype(BF)


def beside_lines(lines, halo):
    columns = dot(lines, halo[...]).astype(BF)
    low = iota((C, LANES), 1) < 64
    at_left, at_right = lane_masks()
    rows = jnp.where(low, lines[:, 0:LANES], pltpu.roll(lines[:, LANES:], 64, 1))
    none = jnp.zeros_like(rows)
    moved = (
        jnp.where(at_left, none, pltpu.roll(rows, 1, 1)),
        rows,
        jnp.where(at_right, none, pltpu.roll(rows, LANES - 1, 1)),
    )
    parts = [
        jnp.concatenate([moved[s], columns[:, s * LANES : (s + 1) * LANES]], axis=1) for s in range(3)
    ]
    return jnp.concatenate(parts, axis=0)


def half_shift(dst, ref, before, after):
    low = iota((C, LANES), 1) < 64
    for t in range(TILES + 1):
        here = tile(ref, t) if t < TILES else after
        prev = tile(ref, t - 1) if t > 0 else before
        mixed = jnp.where(low, here.astype(F32), prev.astype(F32))
        dst[:, t * LANES : (t + 1) * LANES] = pltpu.roll(mixed, 64, 1).astype(BF)


def stack_of(half, ref, start, width):
    at = start * LANES
    size = width * LANES
    return jnp.concatenate(
        [half[:, at : at + size], ref[:, at : at + size], half[:, at + LANES : at + LANES + size]], axis=0
    )


def conv_tiles(weights, half, ref, columns, visit):
    at_left, at_right = lane_masks()
    for chunk in range(TILES // 2):
        taps = dot(weights, stack_of(half, ref, 2 * chunk, 2))
        for part in range(2):
            t = 2 * chunk + part
            lanes = slice(part * LANES, (part + 1) * LANES)
            side = 0.0 if columns is None else pltpu.roll(columns, (LANES - 2 * t) % LANES, 1)
            left = jnp.where(at_left, side, pltpu.roll(taps[0:C, lanes], 1, 1))
            right = jnp.where(at_right, side, pltpu.roll(taps[2 * C : 3 * C, lanes], LANES - 1, 1))
            visit(t, taps[C : 2 * C, lanes] + left + right)


def block_rows(taps, order):
    return jnp.concatenate([jnp.concatenate([taps[t] for t in row], axis=1) for row in order], axis=0)


def forward_form(taps):
    return block_rows(taps, [[b, 3 + b, 6 + b] for b in range(3)]).astype(BF)


def backward_form(taps):
    return block_rows(taps, [[8 - 3 * a - b for b in range(3)] for a in range(3)]).T.astype(BF)


def row_form(taps):
    return block_rows(taps, [[0, 1, 2], [6, 7, 8]]).astype(BF)


def return_form(taps):
    order = [[tap_of((edge + 2) % 4, step)] for edge in range(4) for step in range(3)]
    return block_rows(taps, order).T.astype(BF)


def float_taps(ref):
    return [ref[t].astype(F32) for t in range(9)]


def column(bias):
    row = jnp.broadcast_to(bias[...], (C, C))
    eye = iota((C, C), 0) == iota((C, C), 1)
    return jnp.broadcast_to(jnp.sum(jnp.where(eye, row, 0.0), axis=1, keepdims=True), (C, LANES))


def prepare_kernel(
    spaces, tables_hbm, rules_hbm, x_ref, g_ref, w1_ref, w2_ref, b1_ref, b2_ref,
    d_act, pre_in, x_side, route, halo, w_edge, back2, b1_out, b2_out,
    half, tables, rules, table_sem,
):
    fetches = [
        pltpu.make_async_copy(tables_hbm, tables, table_sem.at[0]),
        pltpu.make_async_copy(rules_hbm, rules, table_sem.at[1]),
    ]
    for fetch in fetches:
        fetch.start()
    me = lax.axis_index("space")
    taps1 = float_taps(w1_ref)
    taps2 = float_taps(w2_ref)
    wf1 = forward_form(taps1)
    w_edge[0 : 2 * C] = row_form(taps1)
    w_edge[2 * C :] = jnp.concatenate([wf1[0:C], wf1[2 * C : 3 * C]], axis=0)
    back2[...] = return_form(taps2)
    b1_out[...] = column(b1_ref)
    b2_out[...] = column(b2_ref)
    zero = jnp.zeros((C, LANES), BF)
    half_shift(half, g_ref, zero, zero)

    def keep(ref):
        def visit(t, value):
            ref[:, t * LANES : (t + 1) * LANES] = value

        return visit

    conv_tiles(backward_form(taps2), half, g_ref, None, keep(d_act))
    half_shift(half, x_ref, zero, zero)
    conv_tiles(wf1, half, x_ref, None, keep(pre_in))
    at_left, at_right = lane_masks()
    for t in range(TILES):
        at = slice(t * LANES, (t + 1) * LANES)
        x = tile(x_ref, t).astype(F32)
        x_side[0:C, at] = jnp.where(at_left, 0.0, pltpu.roll(x, 1, 1)).astype(BF)
        x_side[C : 2 * C, at] = jnp.where(at_right, 0.0, pltpu.roll(x, LANES - 1, 1)).astype(BF)
    for fetch in fetches:
        fetch.wait()
    for edge in range(4):
        for step in range(3):
            route[edge, :, step * 256 : (step + 1) * 256] = user_matrix(tables, rules, me, spaces, edge, step)
    for step in range(3):
        halo[:, step * LANES : (step + 1) * LANES] = halo_matrix(rules, me, step)


def edge_terms(w_sides, w_rows, stacked):
    rows = dot(w_rows, stacked[:, 0:LANES])
    sides = dot(w_sides, stacked[:, LANES:])
    lane = iota((C, LANES), 1)
    rows = jnp.where(lane < 64, rows[0:C], rows[C : 2 * C])
    return rows, jnp.where((lane & 1) == 0, sides[0:C], sides[C : 2 * C])


def add_edges(t, value, rows, sides):
    at_left, at_right = lane_masks()
    low = iota((C, LANES), 1) < 64
    value = value + jnp.where(at_left | at_right, pltpu.roll(sides, (LANES - 2 * t) % LANES, 1), 0.0)
    if t == 0:
        value = value + jnp.where(low, rows, 0.0)
    if t == TILES - 1:
        value = value + jnp.where(low, 0.0, rows)
    return value


def users_values(route, borders):
    parts = []
    for edge in range(4):
        moved = dot(borders[edge], route[edge]).astype(BF)
        parts += [moved[:, s * 256 : (s + 1) * 256] for s in range(3)]
    return jnp.concatenate(parts, axis=0)


def middle_kernel(
    spaces, choice, m1, m2, n1, n2, d_act, pre_in, route, halo, w_edge, back, bias,
    act_ref, d_ref, p0, p1, p2, p3, beside_ref, users_ref, act_lines, d_lines,
):
    lines, borders = by_edge(spaces, (m1, m2, n1, n2))
    beside = beside_lines(lines, halo)
    beside_ref[...] = beside
    rows, sides = edge_terms(w_edge[2 * C :], w_edge[0 : 2 * C], beside)
    users = users_values(route, borders)
    users_ref[...] = users
    line_grads = dot(back[...], users)
    d_rows = line_grads[:, 0:LANES]
    d_sides = line_grads[:, LANES : 2 * LANES]
    bias_now = bias[...]
    act_edges = []
    d_edges = []
    ends = {}
    for t in range(TILES):
        at = slice(t * LANES, (t + 1) * LANES)
        pre = add_edges(t, pre_in[:, at], rows, sides) + bias_now
        square = pre * pre
        inner = 0.7978845608028654 * pre * (1.0 + 0.044715 * square)
        wave = jnp.tanh(inner)
        cdf = 0.5 + 0.5 * wave
        slope = cdf + 0.5 * pre * (1.0 - wave * wave) * (0.7978845608028654 + 0.1070322243 * square)
        grad = add_edges(t, d_act[:, at], d_rows, d_sides)
        act = (pre * cdf).astype(BF)
        d_pre = (grad * slope).astype(BF)
        act_ref[:, at] = act
        d_ref[:, at] = d_pre
        act_edges.append(edge_only(act))
        d_edges.append(edge_only(d_pre))
        if t in (0, TILES - 1):
            ends[t] = (act, d_pre)
    act_l = lines_from(act_edges, ends[0][0], ends[TILES - 1][0])
    d_l = lines_from(d_edges, ends[0][1], ends[TILES - 1][1])
    act_lines[...] = act_l
    d_lines[...] = d_l
    for out, block in zip((p0, p1, p2, p3), send_blocks(choice[...], act_l, d_l)):
        out[...] = block


WIDE = 512
BIAS_AT = 9 * C


def grads_kernel(
    parts, x_ref, g_ref, act_ref, d_ref, x_side, beside, users, act_lines, d_lines,
    mine, other, half_a, half_d, held_one, held_two, near_one, near_two,
):
    zero = jnp.zeros((C, LANES), BF)
    half_shift(half_a, act_ref, zero, zero)
    half_shift(half_d, d_ref, zero, zero)
    width = 4
    at_left, at_right = lane_masks()
    one = jnp.zeros((3 * C, 3 * C), F32)
    two = jnp.zeros((3 * C, 3 * C), F32)
    ones = jnp.zeros((C, LANES), F32)
    twos = jnp.zeros((C, LANES), F32)
    for start in range(0, TILES, width):
        at = slice(start * LANES, (start + width) * LANES)
        g_tiles = [tile(g_ref, t) for t in range(start, start + width)]
        after = [jnp.where(at_right, zero, pltpu.roll(g, LANES - 1, 1)) for g in g_tiles]
        before = [jnp.where(at_left, zero, pltpu.roll(g, 1, 1)) for g in g_tiles]
        g_now = [jnp.concatenate(after, axis=1), g_ref[:, at], jnp.concatenate(before, axis=1)]
        g_now = jnp.concatenate(g_now, axis=0)
        x_now = jnp.concatenate([x_side[0:C, at], x_ref[:, at], x_side[C : 2 * C, at]], axis=0)
        two = two + dot_nt(g_now, stack_of(half_a, act_ref, start, width))
        one = one + dot_nt(stack_of(half_d, d_ref, start, width), x_now)
        for t in range(start, start + width):
            ones = ones + tile(d_ref, t).astype(F32)
            twos = twos + g_tiles[t - start].astype(F32)
    held_one[...] = one
    held_two[...] = two
    line, _ = line_lanes(iota((C, 256), 1))
    d_l = d_lines[...]
    d_by_edge = jnp.concatenate([jnp.where(line == e, d_l, jnp.zeros_like(d_l)) for e in range(4)], axis=0)
    near_one[...] = dot_nt(d_by_edge, beside[...])
    near_two[...] = dot_nt(users[...], act_lines[...])

    def block_one(a, b):
        value = held_one[(2 - a) * C : (3 - a) * C, b * C : (b + 1) * C]
        for edge in range(4):
            for step in range(3):
                if tap_of(edge, step) == 3 * a + b:
                    value = value + near_one[edge * C : (edge + 1) * C, step * C : (step + 1) * C]
        return value

    def block_two(a, b):
        value = held_two[b * C : (b + 1) * C, a * C : (a + 1) * C]
        for edge in range(4):
            for step in range(3):
                if tap_of(edge, step) == 3 * a + b:
                    at = ((edge + 2) % 4) * 3 + step
                    value = value + near_two[at * C : (at + 1) * C, :]
        return value

    def whole(block, bias):
        tail = jnp.broadcast_to(jnp.sum(bias, axis=1, keepdims=True), (C, WIDE - BIAS_AT))
        return jnp.concatenate([block(a, b) for a in range(3) for b in range(3)] + [tail], axis=1)

    first = whole(block_one, ones)
    second = whole(block_two, twos)
    even = (lax.axis_index("space") % 2) == 0
    keep = jnp.where(even, first, second)
    give = jnp.where(even, second, first)
    share = C // parts
    for part in range(parts):
        at = slice(part * share, (part + 1) * share)
        mine[part] = jnp.concatenate([keep[at, j * LANES : (j + 1) * LANES] for j in range(WIDE // LANES)], axis=0)
        other[part] = jnp.concatenate([give[at, j * LANES : (j + 1) * LANES] for j in range(WIDE // LANES)], axis=0)


def inner_kernel(g_ref, d_ref, w_ref, d_in, half):
    zero = jnp.zeros((C, LANES), BF)
    half_shift(half, d_ref, zero, zero)

    def visit(t, value):
        at = slice(t * LANES, (t + 1) * LANES)
        d_in[:, at] = value + g_ref[:, at].astype(F32)

    conv_tiles(backward_form(float_taps(w_ref)), half, d_ref, None, visit)


def partial_kernel(x_ref, act_ref, w1_ref, w2_ref, bias, out, sides, back, half):
    taps = float_taps(w2_ref)
    wf = forward_form(taps)
    sides[0 : 2 * C] = row_form(taps)
    sides[2 * C :] = jnp.concatenate([wf[0:C], wf[2 * C : 3 * C]], axis=0)
    back[...] = return_form(float_taps(w1_ref))
    zero = jnp.zeros((C, LANES), BF)
    half_shift(half, act_ref, zero, zero)
    bias_now = bias[...]

    def visit(t, value):
        at = slice(t * LANES, (t + 1) * LANES)
        out[:, at] = value + bias_now + x_ref[:, at].astype(F32)

    conv_tiles(wf, half, act_ref, None, visit)


def finish_kernel(
    spaces, partial, d_in, m1, m2, n1, n2, halo, route, sides_ref, back,
    out_hbm, grad_in_hbm, out, grad_in, out_sem, grad_in_sem,
):
    lines, borders = by_edge(spaces, (m1, m2, n1, n2))
    rows, sides = edge_terms(sides_ref[2 * C :], sides_ref[0 : 2 * C], beside_lines(lines, halo))
    wide = PIX // CHUNKS
    copies = []

    def finish(src, dst, sem, before, row_terms, side_terms):
        for t in range(TILES):
            at = slice(t * LANES, (t + 1) * LANES)
            src[:, at] = add_edges(t, before[:, at], row_terms, side_terms).astype(BF)
            if (t + 1) % (TILES // CHUNKS) == 0:
                part = t // (TILES // CHUNKS)
                done = slice(part * wide, (part + 1) * wide)
                copies.append(pltpu.make_async_copy(src.at[:, done], dst.at[:, done], sem.at[part]))
                copies[-1].start()

    finish(out, out_hbm, out_sem, partial, rows, sides)
    line_grads = dot(back[...], users_values(route, borders))
    finish(grad_in, grad_in_hbm, grad_in_sem, d_in, line_grads[:, 0:LANES], line_grads[:, LANES:])
    for copy in copies:
        copy.wait()


def unpack_kernel(share, own, got, grad_one, bias_one, grad_two, bias_two):
    even = (lax.axis_index("space") % 2) == 0
    one = jnp.where(even, own[...], got[...])
    two = jnp.where(even, got[...], own[...])
    first, second = [
        jnp.concatenate([value[j * share : (j + 1) * share] for j in range(WIDE // LANES)], axis=1)
        for value in (one, two)
    ]
    eye = iota((share, LANES), 0) == iota((share, LANES), 1)
    for value, grad, bias in ((first, grad_one, bias_one), (second, grad_two, bias_two)):
        for tap in range(9):
            grad[tap] = value[:, tap * C : (tap + 1) * C]
        tail = jnp.broadcast_to(value[:, BIAS_AT : BIAS_AT + 1], (share, LANES))
        bias[...] = jnp.sum(jnp.where(eye, tail, 0.0), axis=0, keepdims=True)[:, 0:share]


def call(kernel, outs, specs, args, scratch=(), read=0, out_specs=None):
    return pl.pallas_call(
        kernel,
        out_shape=[jax.ShapeDtypeStruct(shape, dtype) for shape, dtype in outs],
        in_specs=specs,
        out_specs=out_specs or [VMEM] * len(outs),
        scratch_shapes=list(scratch),
        compiler_params=pltpu.CompilerParams(vmem_limit_bytes=16 * 2**20),
        cost_estimate=pl.CostEstimate(flops=0, bytes_accessed=read, transcendentals=0),
    )(*args)


HBM = pl.BlockSpec(memory_space=pltpu.HBM)


def in_hbm(value):
    return pltpu.with_memory_space_constraint(value, pltpu.HBM)


def swapped(block, mask, devices):
    return lax.ppermute(block, ("dp", "space"), [(i, i ^ mask) for i in range(devices)])


def swap_along(blocks, spaces, more=1):
    def second(i):
        return (i - 1) % spaces if i % 2 == 0 else (i + 1) % spaces

    return [
        lax.ppermute(blocks[0], "space", [(i, i ^ 1) for i in range(spaces)]),
        lax.ppermute(jnp.concatenate([blocks[1]] * more, axis=0) if more > 1 else blocks[1], "space", [(i, second(i)) for i in range(spaces)]),
    ]


def swap_across(blocks, spaces, devices):
    hop = spaces // 4
    return [swapped(blocks[0], hop, devices), swapped(blocks[1], hop ^ 2 * hop, devices)]


def first_rounds(parts, spaces):
    rounds = [[(True, 1 << bit)] for bit in reversed(range(parts.bit_length() - 1))]
    bit = 2
    while bit < spaces // 4:
        single = [r for r in rounds if len(r) == 1]
        if single:
            single[0].append((False, bit))
        else:
            rounds.append([(False, bit)])
        bit *= 2
    return rounds


def total_of(a, b, c, d):
    return (a.astype(F32) + b.astype(F32)) + (c.astype(F32) + d.astype(F32))


def last_round(held, blocks, spaces, devices, others):
    hop = spaces // 4
    held = held.astype(BF)
    joined = [jnp.concatenate([block, held], axis=0) for block in blocks]
    near, far = swap_across(joined, spaces, devices)
    opposite = swapped(held, 2 * hop, devices)
    held, *others = lax.optimization_barrier((held, *others))
    return near, far, total_of(held, near[C:], opposite, far[C:]), others


def reduced(held, bits, devices, spaces):
    where = lax.axis_index("dp")
    keep = give = held.astype(BF)
    masks = []
    for is_part, bit in bits:
        masks.append(bit * spaces if is_part else bit)
        if is_part:
            upper = (where // bit) % 2 == 1
            low, high = keep[: keep.shape[0] // 2], keep[keep.shape[0] // 2 :]
            keep, give = jnp.where(upper, high, low), jnp.where(upper, low, high)
    first = swapped(give, masks[0], devices)
    if len(masks) == 1:
        return keep.astype(F32) + first.astype(F32)
    return total_of(keep, first, swapped(keep, masks[1], devices), swapped(give, masks[0] ^ masks[1], devices))


COST = 3_690_000


def on_device(inputs, cotangent, conv_one, bias_one, conv_two, bias_two, neighbours, corner_rule):
    parts = lax.axis_size("dp")
    spaces = lax.axis_size("space")
    share = C // parts
    x = inputs.reshape(C, PIX)
    g = cotangent.reshape(C, PIX)
    line = ((C, LANES), BF)
    image = ((C, PIX), BF)
    wide = ((C, PIX), F32)
    half = pltpu.VMEM((C, PIX + LANES), BF)
    tables = neighbours.transpose(2, 1, 0)
    rules = corner_rule.transpose(1, 0)

    bias = ((C, LANES), F32)
    *sent, x_near, g_near, choice = call(
        functools.partial(send_kernel, spaces), [line] * 4 + [image, image, ((256, 512), BF)], [HBM] * 3, (in_hbm(tables), in_hbm(x), in_hbm(g)),
        [pltpu.SMEM(tables.shape, jnp.int32), pltpu.SemaphoreType.DMA, pltpu.SemaphoreType.DMA((CHUNKS,)),
         pltpu.SemaphoreType.DMA((CHUNKS,))],
        read=COST * 2,
    )
    devices = parts * spaces
    arrived = swap_along(sent[:2], spaces, 2) + swap_across(sent[2:], spaces, devices)
    edges = ((4 * C, 3 * C), BF)
    back = ((C, 12 * C), BF)
    d_act, pre_in, x_side, route, halo, w_edge, back2, b_one, b_two = call(
        functools.partial(prepare_kernel, spaces),
        [wide, wide, ((2 * C, PIX), BF), ((4, SIDE, 768), BF), ((256, 384), BF), edges, back,
         bias, bias],
        [HBM, HBM] + [VMEM] * 6,
        (in_hbm(tables), in_hbm(rules), x_near, g_near, conv_one, conv_two, bias_one.reshape(1, C), bias_two.reshape(1, C)),
        [half, pltpu.SMEM(tables.shape, jnp.int32), pltpu.SMEM(rules.shape, jnp.int32), pltpu.SemaphoreType.DMA((2,))],
        read=COST * 3,
    )
    middle = call(
        functools.partial(middle_kernel, spaces),
        [image, image] + [line] * 4 + [((3 * C, 256), BF), ((12 * C, 256), BF), ((C, 256), BF), ((C, 256), BF)],
        [VMEM] * 12,
        (choice, *arrived, d_act, pre_in, route, halo, w_edge, back2, b_one),
        read=COST * 9 // 4,
    )
    act, d_pre = middle[:2]
    beside, users, act_lines, d_lines = middle[6:]
    packed = ((parts, share * WIDE // LANES, LANES), F32)
    mine, other = call(
        functools.partial(grads_kernel, parts), [packed, packed], [VMEM] * 9,
        (x, g, act, d_pre, x_side, beside, users, act_lines, d_lines),
        [half, half, pltpu.VMEM((3 * C, 3 * C), F32), pltpu.VMEM((3 * C, 3 * C), F32),
         pltpu.VMEM((4 * C, 3 * C), F32), pltpu.VMEM((12 * C, C), F32)],
        read=COST * 5 // 4,
    )
    blocks = middle[2:6]
    again = swap_along(blocks[:2], spaces, 3)
    act_late, d_late, *again = lax.optimization_barrier((act, d_pre, *again))
    (d_in,) = call(inner_kernel, [wide], [VMEM] * 3, (g, d_late, conv_one), [half], read=COST)
    partial, edges_two, back_one = call(
        partial_kernel, [wide, edges, back], [VMEM] * 5, (x, act_late, conv_one, conv_two, b_two), [half], read=COST * 3 // 2
    )
    held = mine + swapped(other, 1, devices)
    for bits in first_rounds(parts, spaces):
        held = reduced(held, bits, devices, spaces)
    near, far, own, (partial, d_in) = last_round(held[0], blocks[2:], spaces, devices, (partial, d_in))
    got = swapped(own, 1, devices)
    output, grad_in = call(
        functools.partial(finish_kernel, spaces), [image, image], [VMEM] * 10,
        (partial, d_in, *again, near, far, halo, route, edges_two, back_one),
        [pltpu.VMEM((C, PIX), BF), pltpu.VMEM((C, PIX), BF), pltpu.SemaphoreType.DMA((CHUNKS,)),
         pltpu.SemaphoreType.DMA((CHUNKS,))],
        read=COST * 3 // 2, out_specs=[HBM, HBM],
    )
    taps = ((9, share, C), F32)
    bias = ((1, share), F32)
    grad_one, sum_one, grad_two, sum_two = call(
        functools.partial(unpack_kernel, share), [taps, bias, taps, bias], [VMEM] * 2, (own, got), read=10**5
    )
    shape = inputs.shape
    return (
        output.reshape(shape),
        grad_in.reshape(shape),
        grad_one,
        sum_one.reshape(share),
        grad_two,
        sum_two.reshape(share),
    )


def solution(mesh):
    tiles = P("dp", "space", None, None)
    return jax.shard_map(
        on_device,
        mesh=mesh,
        in_specs=(tiles, tiles, P(), P(), P(), P(), P(), P()),
        out_specs=(tiles, tiles, P(None, "dp", None), P("dp"), P(None, "dp", None), P("dp")),
        check_vma=False,
    )
```
